32 devices in a mesh: ctx: 16 (over z, y, x), head: 2 (over core).
Axes of the slice: x: 2, y: 2, z: 4, core: 2. Of those that a mesh axis runs over, the one named last changes fastest.
Arguments:
- lin_query: bfloat16 [2048, 64, 128], P('ctx', 'head'), may hold values from -6 to 6
- lin_key: bfloat16 [2048, 64, 128], P('ctx', 'head'), may hold values from -6 to 6
- lin_value: bfloat16 [2048, 64, 128], P('ctx', 'head'), may hold values from -18 to 18
- log_decay: float32 [64, 2048], P('head', 'ctx'), may hold values from -1 to 0
- norm_gain: float32 [64, 128], P('head'), may hold values from 0.5 to 1.5
- attn_query: bfloat16 [2048, 64, 128], P('ctx', 'head'), may hold values from -30 to 30
- attn_key: bfloat16 [2048, 8, 128], P('ctx', 'head'), may hold values from -16 to 16
- attn_value: bfloat16 [2048, 8, 128], P('ctx', 'head'), may hold values from -6 to 6
Outputs:
- lin_out: bfloat16 [2048, 64, 128], P('ctx', 'head')
- attn_out: bfloat16 [2048, 64, 128], P('ctx', 'head')
The draws below stay inside these ranges and needn't reach their ends.
All inputs are finite; a program needn't handle non-finite values.
Results may differ from the reference program's by a relative error of at most 0.0055.
Values may be sent and summed in bfloat16 or wider, within the bound.
A program may use at most 192 MiB of HBM per device.

```python
import math
import jax
import jax.numpy as jnp
from jax import lax

QUERY_HEADS = 64
HD = 128
KV = 8
TOK_DEV = 128
SEQUENCE_LENGTH = 2048


def draw_lin_value(key, part):
    head_rank = jnp.arange(QUERY_HEADS, dtype=jnp.float32) / max(QUERY_HEADS - 1, 1)
    noise_base = jnp.clip(jax.random.normal(key, (SEQUENCE_LENGTH, QUERY_HEADS, HD), jnp.float32), -6.0, 6.0)
    head_scale = jnp.exp(math.log(3.0) * head_rank)
    return (noise_base * head_scale[None, :, None]).astype(jnp.bfloat16)


def draw_log_decay(key, part):
    key_sequence = jax.random.split(key, 6)
    slow_share = 0.5
    slow_heads = jax.random.uniform(key_sequence[0], (QUERY_HEADS,), jnp.float32) < slow_share
    fast_rate = jnp.exp(jax.random.uniform(key_sequence[1], (QUERY_HEADS,), jnp.float32, math.log(1.0 / 50.0), math.log(1.0 / 30.0)))
    slow_rate = jnp.exp(jax.random.uniform(key_sequence[2], (QUERY_HEADS,), jnp.float32, math.log(0.1), math.log(0.6))) / SEQUENCE_LENGTH
    per_head_decay = jnp.where(slow_heads, slow_rate, fast_rate)
    block_factor = jnp.exp(jax.random.uniform(key_sequence[3], (QUERY_HEADS, SEQUENCE_LENGTH // TOK_DEV), jnp.float32, math.log(0.7), math.log(1.4)))
    position_weight = jnp.repeat(block_factor, TOK_DEV, axis=1)
    spike_location = jax.random.randint(key_sequence[4], (QUERY_HEADS, 2), 0, SEQUENCE_LENGTH)
    token_position = jnp.arange(SEQUENCE_LENGTH)
    spike_found = jnp.any(token_position[None, None, :] == spike_location[:, :, None], axis=1)
    spike_penalty = jnp.log(jax.random.uniform(key_sequence[5], (QUERY_HEADS, SEQUENCE_LENGTH), jnp.float32, 0.5, 0.8))
    return (-per_head_decay[:, None] * position_weight + jnp.where(spike_found, spike_penalty, 0.0)).astype(jnp.float32)


def attention_pair(key):
    query_shape = (SEQUENCE_LENGTH, QUERY_HEADS, HD)
    key_shape = (SEQUENCE_LENGTH, KV, HD)
    query_base = jnp.clip(jax.random.normal(jax.random.fold_in(key, 13), query_shape, jnp.float32), -6.0, 6.0)
    key_base = 2.5 * jnp.clip(jax.random.normal(jax.random.fold_in(key, 11), key_shape, jnp.float32), -6.0, 6.0)
    return (query_base, key_base)


def draw_attn_query(key, part):
    return attention_pair(key)[0].astype(jnp.bfloat16)


def draw_attn_key(key, part):
    return attention_pair(key)[1].astype(jnp.bfloat16)


def shard_levels(key, shape, pieces, low, top_value):
    gain = 1.0
    for position, blocks in pieces:
        draws = jax.random.uniform(jax.random.fold_in(jax.random.fold_in(key, 6), position), (blocks,), jnp.float32, low / len(pieces), top_value / len(pieces))
        gain = gain * jnp.repeat(jnp.exp(draws), shape[position] // blocks).reshape((-1,) + (1,) * (len(shape) - 1 - position))
    return gain


def gaussian(rng, dims, deviation, bound, cuts=(), kind=jnp.bfloat16):
    loudness = shard_levels(rng, dims, cuts, -0.22, 0.18) if cuts else 1.0
    drawn = jax.random.normal(rng, dims, jnp.float32) * deviation * loudness
    return jnp.minimum(jnp.maximum(drawn, -bound), bound).astype(kind)


def setup_inputs(seed: int = 0) -> dict:
    arg_keys = jax.random.split(jax.random.key(seed), 9)
    lin_query = gaussian(arg_keys[0], (SEQUENCE_LENGTH, QUERY_HEADS, HD), 1.0, 6.0, ((0, 16), (1, 2)))
    lin_key = gaussian(arg_keys[1], (SEQUENCE_LENGTH, QUERY_HEADS, HD), 1.0, 6.0, ((0, 16), (1, 2)))
    lin_value = draw_lin_value(jax.random.fold_in(arg_keys[8], 71), 0)
    log_decay = draw_log_decay(jax.random.fold_in(arg_keys[8], 71), 0)
    norm_gain = jnp.clip(1.0 + 0.1 * jax.random.normal(arg_keys[4], (QUERY_HEADS, HD), jnp.float32), 0.5, 1.5)
    attn_query = draw_attn_query(jax.random.fold_in(arg_keys[8], 71), 0)
    attn_key = draw_attn_key(jax.random.fold_in(arg_keys[8], 71), 0)
    attn_value = gaussian(arg_keys[7], (SEQUENCE_LENGTH, KV, HD), 1.0, 6.0, ((0, 16), (1, 2)))
    return {"lin_query": lin_query, "lin_key": lin_key, "lin_value": lin_value, "log_decay": log_decay, "norm_gain": norm_gain, "attn_query": attn_query, "attn_key": attn_key, "attn_value": attn_value}


def round_half(values):
    return lax.optimization_barrier(values.astype(jnp.bfloat16)).astype(jnp.float32)

def act_round(values):
    return round_half(jax.nn.silu(values.astype(jnp.float32)))

def lightning_block(state_now, block_in):
    query_blk, key_blk, value_blk, decay_blk = block_in
    act_query = act_round(query_blk)
    act_key = act_round(key_blk)
    act_value = act_round(value_blk)
    cumulative = jnp.cumsum(decay_blk, axis=1)
    token_position = jnp.arange(query_blk.shape[0])
    causal = token_position[:, None] >= token_position[None, :]
    spread = cumulative[:, :, None] - cumulative[:, None, :]
    decay_matrix = jnp.exp(jnp.where(causal[None], spread, -1e+30))
    scores = jnp.einsum('thd,shd->hts', act_query, act_key, precision=lax.Precision.HIGHEST)
    weights = round_half(scores * decay_matrix)
    inner_part = jnp.einsum('hts,shd->thd', weights, act_value, precision=lax.Precision.HIGHEST)
    last_sum = cumulative[:, -1]
    key_factor = jnp.exp(last_sum[None, :] - cumulative.T)
    scaled_keys = round_half(act_key * key_factor[:, :, None])
    local_state = jnp.einsum('shd,she->hde', scaled_keys, act_value, precision=lax.Precision.HIGHEST)
    outer_part = jnp.einsum('thd,hde->the', act_query, state_now, precision=lax.Precision.HIGHEST)
    mixed_out = inner_part + outer_part * jnp.exp(cumulative.T)[:, :, None]
    state_next = jnp.exp(last_sum)[:, None, None] * state_now + local_state
    return (state_next, mixed_out)

def lightning_layer(lin_query, lin_key, lin_value, log_decay, norm_gain):
    blocks = SEQUENCE_LENGTH // TOK_DEV
    shaped = (blocks, TOK_DEV, QUERY_HEADS, HD)
    decay_blocks = log_decay.reshape(QUERY_HEADS, blocks, TOK_DEV).transpose(1, 0, 2)
    start_state = jnp.zeros((QUERY_HEADS, HD, HD), jnp.float32)
    final_state, mixed_out = lax.scan(lightning_block, start_state, (lin_query.reshape(shaped), lin_key.reshape(shaped), lin_value.reshape(shaped), decay_blocks))
    mixed_out = mixed_out.reshape(SEQUENCE_LENGTH, QUERY_HEADS, HD)
    mean_square = lax.optimization_barrier(jnp.sum(mixed_out * mixed_out, axis=(1, 2))) / (QUERY_HEADS * HD)
    inverse = lax.rsqrt(mean_square + 1e-06)
    return (mixed_out * inverse[:, None, None] * norm_gain[None]).astype(jnp.bfloat16)

def softmax_layer(attn_query, attn_key, attn_value):
    group = QUERY_HEADS // KV
    block_rows = 64
    keys_full = attn_key.astype(jnp.float32)
    values_full = attn_value.astype(jnp.float32)
    key_pos = jnp.arange(SEQUENCE_LENGTH)

    def one_block(block_start):
        query_blk = lax.dynamic_slice_in_dim(attn_query, block_start, block_rows, 0)
        query_blk = query_blk.astype(jnp.float32).reshape(block_rows, KV, group, HD)
        scores = jnp.einsum('bgrd,sgd->bgrs', query_blk, keys_full, precision=lax.Precision.HIGHEST) * HD ** (-0.5)
        query_pos = block_start + jnp.arange(block_rows)
        visible = query_pos[:, None] >= key_pos[None, :]
        masked = jnp.where(visible[:, None, None, :], scores, -1e+30)
        running_max = lax.optimization_barrier(jnp.max(masked, axis=3))
        prob_rows = jnp.where(visible[:, None, None, :], jnp.exp(scores - running_max[..., None]), 0.0)
        totals = lax.optimization_barrier(jnp.sum(prob_rows, axis=3))
        prob_rounded = round_half(prob_rows)
        summed = jnp.einsum('bgrs,sgd->bgrd', prob_rounded, values_full, precision=lax.Precision.HIGHEST)
        return (summed / totals[..., None]).reshape(block_rows, QUERY_HEADS, HD)
    starts = (jnp.arange(SEQUENCE_LENGTH // block_rows) * block_rows).astype(jnp.int32)
    outputs = lax.map(one_block, starts)
    return outputs.reshape(SEQUENCE_LENGTH, QUERY_HEADS, HD).astype(jnp.bfloat16)

def reference(lin_query, lin_key, lin_value, log_decay, norm_gain, attn_query, attn_key, attn_value):
    lin_out = lightning_layer(lin_query, lin_key, lin_value, log_decay, norm_gain)
    attn_out = softmax_layer(attn_query, attn_key, attn_value)
    return (lin_out, attn_out)
```

```python
import functools
import math

import jax
import jax.numpy as jnp
from jax import lax
from jax.experimental import pallas as pl
from jax.experimental.pallas import tpu as pltpu
from jax.sharding import PartitionSpec as P

QUERY_HEADS = 64
HD = 128
GROUP = 4
F32 = jnp.float32
BF16 = jnp.bfloat16
MESH = pl.DeviceIdType.MESH
NT = (((1,), (1,)), ((), ()))
TN = (((0,), (0,)), ((), ()))
MQ = 256


def silu(x):
    return x / (1.0 + jnp.exp(-x))


def kernel(
    planes, heads_dev, lq, lk, lv, decay, gain, aq, kv_in, lin_out, attn_out,
    qf, kf, vf, mixed, kv, qs, acc, m_ref, l_ref, ot, cum_ref, lastb,
    sbuf, rs, prior, pr_send, carry, carry_out, rowsq, rowsq_in,
    z_s, z_r, x_s, x_r, y_s, y_r, dk_s, dk_r, dv_s, dv_r,
    s1_s, s1_r, la_s, la_r, s3_s, s3_r, c_s, c_r, h_s, h_r,
):
    rows, heads, _ = lq.shape
    kv_local = kv_in.shape[1]
    group = heads // kv_local
    quarter = heads // GROUP
    me = lax.axis_index("ctx")
    my_head = lax.axis_index("head")
    z = me // GROUP
    p = me % GROUP
    base = z * GROUP
    px = jnp.where(p % 2 == 0, p + 1, p - 1)
    py = (p + 2) % GROUP
    pd = jnp.where(px >= 2, px - 2, px + 2)
    peers = (px, py, pd)
    has_up = z < planes - 1
    has_down = z > 0

    def remote(src, dst, s, r, ctx):
        return pltpu.make_async_remote_copy(
            src_ref=src, dst_ref=dst, send_sem=s, recv_sem=r,
            device_id={"ctx": ctx}, device_id_type=MESH,
        )

    kv[:, :, z, p] = kv_in[...]

    barrier = pltpu.get_barrier_semaphore()
    for peer in peers:
        pl.semaphore_signal(barrier, inc=1, device_id={"ctx": base + peer}, device_id_type=MESH)
    for j in range(1, heads_dev):
        pl.semaphore_signal(
            barrier, inc=1, device_id={"head": (my_head + j) % heads_dev}, device_id_type=MESH
        )

    @pl.when(has_up)
    def _():
        pl.semaphore_signal(barrier, inc=1, device_id={"ctx": me + GROUP}, device_id_type=MESH)

    @pl.when(has_down)
    def _():
        pl.semaphore_signal(barrier, inc=1, device_id={"ctx": me - GROUP}, device_id_type=MESH)

    along = jnp.where(has_up, 1, 0) + jnp.where(has_down, 1, 0)
    pl.semaphore_wait(barrier, GROUP - 1 + heads_dev - 1 + along)

    def block(zz, col):
        return kv.at[:, :, zz, col]

    def up_copy(zz):
        return remote(block(zz, p), block(zz, p), z_s.at[zz], z_r.at[zz], me + GROUP)

    def x_copy(zz, col):
        return remote(block(zz, col), block(zz, col), x_s.at[zz], x_r.at[zz], base + px)

    def y_copy(zz, col):
        return remote(block(zz, col), block(zz, col), y_s.at[zz], y_r.at[zz], base + py)

    def dk_copy(zz, col):
        return remote(
            kv.at[0, :, zz, col], kv.at[0, :, zz, col], dk_s.at[zz], dk_r.at[zz], base + py
        )

    def dv_copy(zz, col):
        return remote(
            kv.at[1, :, zz, col], kv.at[1, :, zz, col], dv_s.at[zz], dv_r.at[zz], base + px
        )

    def send_column(zz):
        @pl.when(has_up)
        def _():
            up_copy(zz).start()

        x_copy(zz, p).start()
        y_copy(zz, p).start()

    send_column(z)

    step = 16

    def activate(src, dst):
        def body(i, _):
            t0 = pl.multiple_of(i * step, step)
            x = silu(src[pl.ds(t0, step)].astype(F32))
            r0 = pl.multiple_of(t0 * heads, step * heads)
            dst[pl.ds(r0, step * heads), :] = x.reshape(step * heads, HD)
            return 0

        lax.fori_loop(0, rows // step, body, 0)

    def head_rows(ref, h):
        return ref[pl.ds(h, rows, stride=heads), :]

    row_id = lax.broadcasted_iota(jnp.int32, (rows, rows), 0)
    col_id = lax.broadcasted_iota(jnp.int32, (rows, rows), 1)
    upper = jnp.where(row_id <= col_id, 1.0, 0.0).astype(F32)
    cum_all = lax.dot_general(
        decay[...], upper, (((1,), (0,)), ((), ())),
        precision=lax.Precision.HIGHEST, preferred_element_type=F32,
    )
    cum_ref[...] = cum_all
    lastb[p] = jnp.broadcast_to(cum_all[:, rows - 1 : rows], (heads, HD))
    last_copies = [
        remote(lastb.at[p], lastb.at[p], la_s.at[i], la_r.at[i], base + peer)
        for i, peer in enumerate(peers)
    ]
    for c in last_copies:
        c.start()

    activate(lk, kf)
    activate(lv, vf)

    def cum_of(h):
        row = jnp.broadcast_to(cum_ref[pl.ds(h, 1), :], (rows, rows))
        return row, row.T

    def local_state(h, _):
        row, col = cum_of(h)
        last = jnp.broadcast_to(lastb[p, pl.ds(h, 1), :], (rows, HD))
        sk = (head_rows(kf, h).astype(BF16).astype(F32) * jnp.exp(last - col)).astype(BF16)
        v = head_rows(vf, h).astype(BF16)
        st = lax.dot_general(sk, v, TN, preferred_element_type=F32)
        sbuf[h // quarter, h % quarter] = st.astype(BF16)
        return 0

    lax.fori_loop(0, heads, local_state, 0)

    s1 = [
        remote(sbuf.at[peer], rs.at[p], s1_s.at[i], s1_r.at[i], base + peer)
        for i, peer in enumerate(peers)
    ]
    for c in s1:
        c.start()

    def load_queries(i, _):
        t0 = pl.multiple_of(i * step, step)
        x = aq[pl.ds(t0, step)].astype(F32)
        for g in range(kv_local):
            part = x[:, g * group : (g + 1) * group, :].reshape(step * group, HD)
            r0 = pl.multiple_of(t0 * group, step * group)
            qs[g, pl.ds(r0, step * group), :] = part.astype(BF16)
        return 0

    lax.fori_loop(0, rows // step, load_queries, 0)
    activate(lq, qf)

    def inner(h, _):
        row, col = cum_of(h)
        q = head_rows(qf, h).astype(BF16)
        k = head_rows(kf, h).astype(BF16)
        v = head_rows(vf, h).astype(BF16)
        sc = lax.dot_general(q, k, NT, preferred_element_type=F32)
        dm = jnp.exp(jnp.where(row_id >= col_id, col - row, -1e30))
        w = (sc * dm).astype(BF16)
        mixed[pl.ds(h, rows, stride=heads), :] = jnp.dot(w, v, preferred_element_type=F32)
        return 0

    lax.fori_loop(0, heads, inner, 0)

    m_ref[...] = jnp.full(m_ref.shape, -1e30, F32)
    l_ref[...] = jnp.zeros(l_ref.shape, F32)
    acc[...] = jnp.zeros(acc.shape, F32)
    scale = HD ** (-0.5) * math.log2(math.e)
    span = GROUP * rows
    tiles = rows * group // MQ

    def attend(zz, masked):
        def body(i, _):
            g = i // tiles
            q0 = pl.multiple_of((i % tiles) * MQ, MQ)
            cols = pl.ds(q0, MQ)
            k = kv[0, g, zz].reshape(span, HD)
            v = kv[1, g, zz].reshape(span, HD)
            s = lax.dot_general(k, qs[g, cols, :], NT, preferred_element_type=F32) * scale
            if masked:
                key_pos = lax.broadcasted_iota(jnp.int32, (span, MQ), 0)
                q_pos = p * rows + (q0 + lax.broadcasted_iota(jnp.int32, (span, MQ), 1)) // group
                s = jnp.where(key_pos <= q_pos, s, -1e30)
            m_old = m_ref[g, :, cols]
            m_new = jnp.maximum(m_old, jnp.max(s, axis=0, keepdims=True))
            alpha = jnp.exp2(m_old - m_new)
            e = jnp.exp2(s - m_new)
            m_ref[g, :, cols] = m_new
            l_ref[g, :, cols] = l_ref[g, :, cols] * alpha + jnp.sum(e, axis=0, keepdims=True)
            o = lax.dot_general(v, e.astype(BF16), TN, preferred_element_type=F32)
            acc[g, :, cols] = acc[g, :, cols] * alpha + o
            return 0

        lax.fori_loop(0, kv_local * tiles, body, 0)

    def carry_copy():
        return remote(carry_out, carry, c_s, c_r, me + GROUP)

    def state_chain():
        for i in range(GROUP - 1):
            s1[i].wait_recv()
            last_copies[i].wait_recv()
        rs[p] = sbuf[p]

        @pl.when(has_down)
        def _():
            carry_copy().wait_recv()

        @pl.when(jnp.logical_not(has_down))
        def _():
            carry[...] = jnp.zeros(carry.shape, BF16)

        def one(hh, _):
            h = p * quarter + hh
            state = carry[hh].astype(F32)
            for i in range(GROUP):
                pr_send[i, hh] = state.astype(BF16)
                d = jnp.exp(lastb[i, pl.ds(h, 1), :])
                state = d * state + rs[i, hh].astype(F32)
            carry_out[hh] = state.astype(BF16)
            return 0

        lax.fori_loop(0, quarter, one, 0)

        @pl.when(has_up)
        def _():
            carry_copy().start()

        for c in s3:
            c.start()
        prior[p] = pr_send[p]

    s3 = [
        remote(pr_send.at[peer], prior.at[p], s3_s.at[i], s3_r.at[i], base + peer)
        for i, peer in enumerate(peers)
    ]

    def turn(r, _):
        zz = z - r

        @pl.when(r < z)
        def _():
            up_copy(zz - 1).wait_recv()
            send_column(zz - 1)

        @pl.when(r <= z)
        def _():
            x_copy(zz, px).wait_recv()
            dk_copy(zz, px).start()
            y_copy(zz, py).wait_recv()
            dv_copy(zz, py).start()

        @pl.when(r == z + 1)
        def _():
            state_chain()

        @pl.when(r > 0)
        def _():
            dk_copy(zz + 1, pd).wait_recv()
            dv_copy(zz + 1, pd).wait_recv()

        @pl.when(r == 1)
        def _():
            attend(zz + 1, True)

        @pl.when(r > 1)
        def _():
            attend(zz + 1, False)

        return 0

    lax.fori_loop(0, z + 2, turn, 0)

    for c in s3:
        c.wait_recv()
    rowsq[...] = jnp.zeros(rowsq.shape, F32)

    def outer(h, _):
        _, col = cum_of(h)
        q = head_rows(qf, h).astype(BF16)
        o = jnp.dot(q, prior[h // quarter, h % quarter], preferred_element_type=F32)
        mx = head_rows(mixed, h) + o * jnp.exp(col)
        mixed[pl.ds(h, rows, stride=heads), :] = mx
        rowsq[...] += mx * mx
        return 0

    lax.fori_loop(0, heads, outer, 0)
    h_copies = [
        pltpu.make_async_remote_copy(
            src_ref=rowsq, dst_ref=rowsq_in.at[j - 1], send_sem=h_s.at[j - 1],
            recv_sem=h_r.at[j - 1], device_id={"head": (my_head + j) % heads_dev},
            device_id_type=MESH,
        )
        for j in range(1, heads_dev)
    ]
    for c in h_copies:
        c.start()

    for g in range(kv_local):
        for t in range(tiles):
            cols = slice(t * MQ, (t + 1) * MQ)
            ot[g, cols, :] = (acc[g, :, cols] / l_ref[g, :, cols]).T

    def store_attn(i, _):
        t0 = pl.multiple_of(i * step, step)
        r0 = pl.multiple_of(t0 * group, step * group)
        parts = [
            ot[g, pl.ds(r0, step * group), :].reshape(step, group, HD) for g in range(kv_local)
        ]
        attn_out[pl.ds(t0, step)] = jnp.concatenate(parts, axis=1).astype(BF16)
        return 0

    lax.fori_loop(0, rows // step, store_attn, 0)

    for c in h_copies:
        c.wait_recv()
    total = rowsq[...]
    for j in range(heads_dev - 1):
        total = total + rowsq_in[j]
    mean = jnp.sum(total, axis=1, keepdims=True) / (heads_dev * heads * HD)
    for c in h_copies:
        c.wait_send()
    rowsq[...] = jnp.broadcast_to(lax.rsqrt(mean + 1e-06), (rows, HD))

    def store_lin(i, _):
        t0 = pl.multiple_of(i * step, step)
        r0 = pl.multiple_of(t0 * heads, step * heads)
        x = mixed[pl.ds(r0, step * heads), :].reshape(step, heads, HD)
        inv = rowsq[pl.ds(t0, step), :].reshape(step, 1, HD)
        lin_out[pl.ds(t0, step)] = (x * inv * gain[...][None]).astype(BF16)
        return 0

    lax.fori_loop(0, rows // step, store_lin, 0)

    for c in last_copies + s1 + s3:
        c.wait_send()

    @pl.when(has_up)
    def _():
        carry_copy().wait_send()

    def drain(zz, _):
        @pl.when(has_up)
        def _():
            up_copy(zz).wait_send()

        x_copy(zz, p).wait_send()
        y_copy(zz, p).wait_send()
        dk_copy(zz, px).wait_send()
        dv_copy(zz, py).wait_send()
        return 0

    lax.fori_loop(0, z + 1, drain, 0)


def local(planes, heads_dev, lin_query, lin_key, lin_value, log_decay, norm_gain,
          attn_query, attn_key, attn_value):
    rows, heads, _ = lin_query.shape
    kv_local = attn_key.shape[1]
    group = heads // kv_local
    quarter = heads // GROUP
    kv_in = jnp.stack([attn_key.transpose(1, 0, 2), attn_value.transpose(1, 0, 2)])
    vmem = pl.BlockSpec(memory_space=pltpu.VMEM)
    dma = pltpu.SemaphoreType.DMA
    out = jax.ShapeDtypeStruct(lin_query.shape, BF16)
    state = (GROUP, quarter, HD, HD)
    return pl.pallas_call(
        functools.partial(kernel, planes, heads_dev),
        out_shape=(out, out),
        in_specs=[vmem] * 7,
        out_specs=(vmem, vmem),
        scratch_shapes=[
            pltpu.VMEM((rows * heads, HD), F32),
            pltpu.VMEM((rows * heads, HD), F32),
            pltpu.VMEM((rows * heads, HD), F32),
            pltpu.VMEM((rows * heads, HD), F32),
            pltpu.VMEM((2, kv_local, planes, GROUP, rows, HD), BF16),
            pltpu.VMEM((kv_local, rows * group, HD), BF16),
            pltpu.VMEM((kv_local, HD, rows * group), F32),
            pltpu.VMEM((kv_local, 1, rows * group), F32),
            pltpu.VMEM((kv_local, 1, rows * group), F32),
            pltpu.VMEM((kv_local, rows * group, HD), F32),
            pltpu.VMEM((heads, rows), F32),
            pltpu.VMEM((GROUP, heads, HD), F32),
            pltpu.VMEM(state, BF16),
            pltpu.VMEM(state, BF16),
            pltpu.VMEM(state, BF16),
            pltpu.VMEM(state, BF16),
            pltpu.VMEM(state[1:], BF16),
            pltpu.VMEM(state[1:], BF16),
            pltpu.VMEM((rows, HD), F32),
            pltpu.VMEM((max(heads_dev - 1, 1), rows, HD), F32),
        ]
        + [dma((planes,))] * 10
        + [dma((GROUP - 1,))] * 6
        + [dma, dma]
        + [dma((max(heads_dev - 1, 1),))] * 2,
        compiler_params=pltpu.CompilerParams(
            collective_id=0, has_side_effects=True, vmem_limit_bytes=56 * 2**20
        ),
        name="mixers",
    )(lin_query, lin_key, lin_value, log_decay, norm_gain, attn_query, kv_in)


def solution(mesh):
    planes = mesh.shape["ctx"] // GROUP
    return jax.shard_map(
        functools.partial(local, planes, mesh.shape["head"]),
        mesh=mesh,
        in_specs=(
            P("ctx", "head", None),
            P("ctx", "head", None),
            P("ctx", "head", None),
            P("head", "ctx"),
            P("head", None),
            P("ctx", "head", None),
            P("ctx", "head", None),
            P("ctx", "head", None),
        ),
        out_specs=(P("ctx", "head", None), P("ctx", "head", None)),
        check_vma=False,
    )
```

```python
import functools
import math

import jax
import jax.numpy as jnp
from jax import lax
from jax.experimental import pallas as pl
from jax.experimental.pallas import tpu as pltpu
from jax.sharding import PartitionSpec as P

QUERY_HEADS = 64
HD = 128
GROUP = 4
F32 = jnp.float32
BF16 = jnp.bfloat16
MESH = pl.DeviceIdType.MESH
NT = (((1,), (1,)), ((), ()))
TN = (((0,), (0,)), ((), ()))
MQ = 256
PARTS = 2


def silu(x):
    half = 0.5 * x
    return half + half * jnp.tanh(half)


def kernel(
    planes, heads_dev, lq, lk, lv, decay, gain, aq, k_in, v_in, lin_out, attn_out,
    qf, kf, vf, mixed, kv, qs, acc, m_ref, l_ref, ot, cum_ref, colb, lastb,
    sbuf, rs, prior, pr_send, carry, carry_out, rowsq, rowsq_in,
    z_s, z_r, x_s, x_r, y_s, y_r, dk_s, dk_r, dv_s, dv_r,
    s1_s, s1_r, la_s, la_r, s3_s, s3_r, c_s, c_r, h_s, h_r,
):
    rows, heads, _ = lq.shape
    kv_local = k_in.shape[0]
    group = heads // kv_local
    quarter = heads // GROUP
    me = lax.axis_index("ctx")
    my_head = lax.axis_index("head")
    z = me // GROUP
    p = me % GROUP
    base = z * GROUP
    px = jnp.where(p % 2 == 0, p + 1, p - 1)
    py = (p + 2) % GROUP
    pd = jnp.where(px >= 2, px - 2, px + 2)
    peers = (px, py, pd)
    has_up = z < planes - 1
    has_down = z > 0

    def remote(src, dst, s, r, ctx):
        return pltpu.make_async_remote_copy(
            src_ref=src, dst_ref=dst, send_sem=s, recv_sem=r,
            device_id={"ctx": ctx}, device_id_type=MESH,
        )

    kv[0, :, z, p] = k_in[...]
    kv[1, :, z, p] = v_in[...]

    barrier = pltpu.get_barrier_semaphore()
    for peer in peers:
        pl.semaphore_signal(barrier, inc=1, device_id={"ctx": base + peer}, device_id_type=MESH)
    for j in range(1, heads_dev):
        pl.semaphore_signal(
            barrier, inc=1, device_id={"head": (my_head + j) % heads_dev}, device_id_type=MESH
        )

    @pl.when(has_up)
    def _():
        pl.semaphore_signal(barrier, inc=1, device_id={"ctx": me + GROUP}, device_id_type=MESH)

    @pl.when(has_down)
    def _():
        pl.semaphore_signal(barrier, inc=1, device_id={"ctx": me - GROUP}, device_id_type=MESH)

    along = jnp.where(has_up, 1, 0) + jnp.where(has_down, 1, 0)
    pl.semaphore_wait(barrier, GROUP - 1 + heads_dev - 1 + along)

    def block(zz, col):
        return kv.at[:, :, zz, col]

    def up_copy(zz):
        return remote(block(zz, p), block(zz, p), z_s.at[zz], z_r.at[zz], me + GROUP)

    def x_copy(zz, col):
        return remote(block(zz, col), block(zz, col), x_s.at[zz], x_r.at[zz], base + px)

    def y_copy(zz, col):
        return remote(block(zz, col), block(zz, col), y_s.at[zz], y_r.at[zz], base + py)

    def dk_copy(zz, col):
        return remote(
            kv.at[0, :, zz, col], kv.at[0, :, zz, col], dk_s.at[zz], dk_r.at[zz], base + py
        )

    def dv_copy(zz, col):
        return remote(
            kv.at[1, :, zz, col], kv.at[1, :, zz, col], dv_s.at[zz], dv_r.at[zz], base + px
        )

    def send_column(zz):
        @pl.when(has_up)
        def _():
            up_copy(zz).start()

        x_copy(zz, p).start()
        y_copy(zz, p).start()

    send_column(z)

    step = 16

    def activate(src, dst):
        def body(i, _):
            t0 = pl.multiple_of(i * step, step)
            x = silu(src[pl.ds(t0, step)].astype(F32))
            r0 = pl.multiple_of(t0 * heads, step * heads)
            dst[pl.ds(r0, step * heads), :] = x.reshape(step * heads, HD)
            return 0

        lax.fori_loop(0, rows // step, body, 0)

    def head_rows(ref, h):
        return ref[pl.ds(h, rows, stride=heads), :]

    row_id = lax.broadcasted_iota(jnp.int32, (rows, rows), 0)
    col_id = lax.broadcasted_iota(jnp.int32, (rows, rows), 1)
    upper = jnp.where(row_id <= col_id, 1.0, 0.0).astype(F32)
    cum_all = lax.dot_general(
        decay[...], upper, (((1,), (0,)), ((), ())),
        precision=lax.Precision.HIGHEST, preferred_element_type=F32,
    )
    cum_ref[...] = cum_all
    lastb[p] = jnp.broadcast_to(cum_all[:, rows - 1 : rows], (heads, HD))
    last_copies = [
        remote(lastb.at[p], lastb.at[p], la_s.at[i], la_r.at[i], base + peer)
        for i, peer in enumerate(peers)
    ]
    for c in last_copies:
        c.start()

    activate(lk, kf)
    activate(lv, vf)

    together = min(4, quarter)

    def cum_row(h):
        return jnp.broadcast_to(cum_ref[pl.ds(h, 1), :], (rows, rows))

    def local_states(owner):
        def body(i, _):
            hs = [i * together + u for u in range(together)]
            ids = [owner * quarter + hh for hh in hs]
            ks = [head_rows(kf, h).astype(BF16).astype(F32) for h in ids]
            vs = [head_rows(vf, h).astype(BF16) for h in ids]
            lasts = [jnp.broadcast_to(lastb[p, pl.ds(h, 1), :], (rows, HD)) for h in ids]
            cols = [cum_row(h).T for h in ids]
            sks = [(k * jnp.exp(a - c)).astype(BF16) for k, a, c in zip(ks, lasts, cols)]
            sts = [
                lax.dot_general(sk, v, TN, preferred_element_type=F32) for sk, v in zip(sks, vs)
            ]
            for h, c in zip(ids, cols):
                colb[h] = c
            for hh, st in zip(hs, sts):
                sbuf[owner, hh] = st.astype(BF16)
            return 0

        lax.fori_loop(0, quarter // together, body, 0)

    s1 = [
        remote(sbuf.at[peer], rs.at[p], s1_s.at[i], s1_r.at[i], base + peer)
        for i, peer in enumerate(peers)
    ]
    for peer, c in zip(peers, s1):
        local_states(peer)
        c.start()
    local_states(p)

    def load_queries(i, _):
        t0 = pl.multiple_of(i * step, step)
        x = aq[pl.ds(t0, step)].astype(F32)
        for g in range(kv_local):
            part = x[:, g * group : (g + 1) * group, :].reshape(step * group, HD)
            r0 = pl.multiple_of(t0 * group, step * group)
            qs[g, pl.ds(r0, step * group), :] = part.astype(BF16)
        return 0

    lax.fori_loop(0, rows // step, load_queries, 0)
    activate(lq, qf)

    def inner(i, _):
        ids = [i * together + u for u in range(together)]
        qh = [head_rows(qf, h).astype(BF16) for h in ids]
        ks = [head_rows(kf, h).astype(BF16) for h in ids]
        vs = [head_rows(vf, h).astype(BF16) for h in ids]
        spread = [colb[h] - cum_row(h) for h in ids]
        sc = [lax.dot_general(q, k, NT, preferred_element_type=F32) for q, k in zip(qh, ks)]
        dm = [jnp.exp(jnp.where(row_id >= col_id, d, -1e30)) for d in spread]
        ws = [(a * d).astype(BF16) for a, d in zip(sc, dm)]
        outs = [jnp.dot(w, v, preferred_element_type=F32) for w, v in zip(ws, vs)]
        for h, o in zip(ids, outs):
            mixed[pl.ds(h, rows, stride=heads), :] = o
        return 0

    lax.fori_loop(0, heads // together, inner, 0)

    m_ref[...] = jnp.full(m_ref.shape, -1e30, F32)
    l_ref[...] = jnp.zeros(l_ref.shape, F32)
    acc[...] = jnp.zeros(acc.shape, F32)
    scale = HD ** (-0.5) * math.log2(math.e)
    span = GROUP * rows
    tiles = rows * group // MQ

    pair = 2
    sets = tiles // pair

    def attend(zz, masked):
        def body(i, _):
            g = i // sets
            starts = [pl.multiple_of(((i % sets) * pair + u) * MQ, MQ) for u in range(pair)]
            cols = [pl.ds(q0, MQ) for q0 in starts]
            k = kv[0, g, zz].reshape(span, HD)
            v = kv[1, g, zz].reshape(span, HD)
            ss = [
                lax.dot_general(k, qs[g, c, :], NT, preferred_element_type=F32) * scale
                for c in cols
            ]
            if masked:
                key_pos = lax.broadcasted_iota(jnp.int32, (span, MQ), 0)
                col_pos = lax.broadcasted_iota(jnp.int32, (span, MQ), 1)
                ss = [
                    jnp.where(key_pos <= p * rows + (q0 + col_pos) // group, x, -1e30)
                    for q0, x in zip(starts, ss)
                ]
            m_old = [m_ref[g, :, c] for c in cols]
            l_old = [l_ref[g, :, c] for c in cols]
            a_old = [acc[g, :, c] for c in cols]
            m_new = [
                jnp.maximum(m, jnp.max(x, axis=0, keepdims=True)) for m, x in zip(m_old, ss)
            ]
            alpha = [jnp.exp2(a - b) for a, b in zip(m_old, m_new)]
            es = [jnp.exp2(x - m) for x, m in zip(ss, m_new)]
            l_new = [
                old * a + jnp.sum(e, axis=0, keepdims=True)
                for old, a, e in zip(l_old, alpha, es)
            ]
            os = [
                lax.dot_general(v, e.astype(BF16), TN, preferred_element_type=F32) for e in es
            ]
            for u, c in enumerate(cols):
                m_ref[g, :, c] = m_new[u]
                l_ref[g, :, c] = l_new[u]
                acc[g, :, c] = a_old[u] * alpha[u] + os[u]
            return 0

        lax.fori_loop(0, kv_local * sets, body, 0)

    part = quarter // PARTS

    def carry_copy(j):
        own = pl.ds(j * part, part)
        return remote(carry_out.at[own], carry.at[own], c_s.at[j], c_r.at[j], me + GROUP)

    def prior_copy(j, i):
        own = pl.ds(j * part, part)
        n = j * (GROUP - 1) + i
        return remote(
            pr_send.at[peers[i], own], prior.at[p, own], s3_s.at[n], s3_r.at[n], base + peers[i]
        )

    def state_chain():
        for i in range(GROUP - 1):
            s1[i].wait_recv()
            last_copies[i].wait_recv()
        rs[p] = sbuf[p]

        @pl.when(jnp.logical_not(has_down))
        def _():
            carry[...] = jnp.zeros(carry.shape, BF16)

        for j in range(PARTS):

            @pl.when(has_down)
            def _():
                carry_copy(j).wait_recv()

            def one(n, _):
                hh = j * part + n
                h = p * quarter + hh
                state = carry[hh].astype(F32)
                for i in range(GROUP):
                    pr_send[i, hh] = state.astype(BF16)
                    d = jnp.exp(lastb[i, pl.ds(h, 1), :])
                    state = d * state + rs[i, hh].astype(F32)
                carry_out[hh] = state.astype(BF16)
                return 0

            lax.fori_loop(0, part, one, 0)

            @pl.when(has_up)
            def _():
                carry_copy(j).start()

            for i in range(GROUP - 1):
                prior_copy(j, i).start()
        prior[p] = pr_send[p]

    def turn(r, _):
        zz = z - r

        @pl.when(r < z)
        def _():
            up_copy(zz - 1).wait_recv()
            send_column(zz - 1)

        @pl.when(r <= z)
        def _():
            x_copy(zz, px).wait_recv()
            dk_copy(zz, px).start()
            y_copy(zz, py).wait_recv()
            dv_copy(zz, py).start()

        @pl.when(r == z + 1)
        def _():
            state_chain()

        @pl.when(r > 0)
        def _():
            dk_copy(zz + 1, pd).wait_recv()
            dv_copy(zz + 1, pd).wait_recv()

        @pl.when(r == 1)
        def _():
            attend(zz + 1, True)

        @pl.when(r > 1)
        def _():
            attend(zz + 1, False)

        return 0

    lax.fori_loop(0, z + 2, turn, 0)

    for g in range(kv_local):
        for t in range(tiles):
            cols = slice(t * MQ, (t + 1) * MQ)
            ot[g, cols, :] = (acc[g, :, cols] / l_ref[g, :, cols]).T

    def store_attn(i, _):
        t0 = pl.multiple_of(i * step, step)
        r0 = pl.multiple_of(t0 * group, step * group)
        parts = [
            ot[g, pl.ds(r0, step * group), :].reshape(step, group, HD) for g in range(kv_local)
        ]
        attn_out[pl.ds(t0, step)] = jnp.concatenate(parts, axis=1).astype(BF16)
        return 0

    lax.fori_loop(0, rows // step, store_attn, 0)

    for j in range(PARTS):
        for i in range(GROUP - 1):
            prior_copy(j, i).wait_recv()
    rowsq[...] = jnp.zeros(rowsq.shape, F32)

    def outer(i, _):
        ids = [i * together + u for u in range(together)]
        qh = [head_rows(qf, h).astype(BF16) for h in ids]
        old = [head_rows(mixed, h) for h in ids]
        ps = [prior[h // quarter, h % quarter] for h in ids]
        os = [jnp.dot(q, x, preferred_element_type=F32) for q, x in zip(qh, ps)]
        new = [a + o * jnp.exp(colb[h]) for a, o, h in zip(old, os, ids)]
        for h, x in zip(ids, new):
            mixed[pl.ds(h, rows, stride=heads), :] = x
        rowsq[...] += sum(x * x for x in new)
        return 0

    lax.fori_loop(0, heads // together, outer, 0)
    h_copies = [
        pltpu.make_async_remote_copy(
            src_ref=rowsq, dst_ref=rowsq_in.at[j - 1], send_sem=h_s.at[j - 1],
            recv_sem=h_r.at[j - 1], device_id={"head": (my_head + j) % heads_dev},
            device_id_type=MESH,
        )
        for j in range(1, heads_dev)
    ]
    for c in h_copies:
        c.start()

    for c in h_copies:
        c.wait_recv()
    total = rowsq[...]
    for j in range(heads_dev - 1):
        total = total + rowsq_in[j]
    mean = jnp.sum(total, axis=1, keepdims=True) / (heads_dev * heads * HD)
    for c in h_copies:
        c.wait_send()
    rowsq[...] = jnp.broadcast_to(lax.rsqrt(mean + 1e-06), (rows, HD))

    def store_lin(i, _):
        t0 = pl.multiple_of(i * step, step)
        r0 = pl.multiple_of(t0 * heads, step * heads)
        x = mixed[pl.ds(r0, step * heads), :].reshape(step, heads, HD)
        inv = rowsq[pl.ds(t0, step), :].reshape(step, 1, HD)
        lin_out[pl.ds(t0, step)] = (x * inv * gain[...][None]).astype(BF16)
        return 0

    lax.fori_loop(0, rows // step, store_lin, 0)

    for c in last_copies + s1:
        c.wait_send()
    for j in range(PARTS):
        for i in range(GROUP - 1):
            prior_copy(j, i).wait_send()

    @pl.when(has_up)
    def _():
        for j in range(PARTS):
            carry_copy(j).wait_send()

    def drain(zz, _):
        @pl.when(has_up)
        def _():
            up_copy(zz).wait_send()

        x_copy(zz, p).wait_send()
        y_copy(zz, p).wait_send()
        dk_copy(zz, px).wait_send()
        dv_copy(zz, py).wait_send()
        return 0

    lax.fori_loop(0, z + 1, drain, 0)


def local(planes, heads_dev, lin_query, lin_key, lin_value, log_decay, norm_gain,
          attn_query, attn_key, attn_value):
    rows, heads, _ = lin_query.shape
    kv_local = attn_key.shape[1]
    group = heads // kv_local
    quarter = heads // GROUP
    vmem = pl.BlockSpec(memory_space=pltpu.VMEM)
    dma = pltpu.SemaphoreType.DMA
    out = jax.ShapeDtypeStruct(lin_query.shape, BF16)
    state = (GROUP, quarter, HD, HD)
    return pl.pallas_call(
        functools.partial(kernel, planes, heads_dev),
        out_shape=(out, out),
        in_specs=[vmem] * 8,
        out_specs=(vmem, vmem),
        scratch_shapes=[
            pltpu.VMEM((rows * heads, HD), F32),
            pltpu.VMEM((rows * heads, HD), F32),
            pltpu.VMEM((rows * heads, HD), F32),
            pltpu.VMEM((rows * heads, HD), F32),
            pltpu.VMEM((2, kv_local, planes, GROUP, rows, HD), BF16),
            pltpu.VMEM((kv_local, rows * group, HD), BF16),
            pltpu.VMEM((kv_local, HD, rows * group), F32),
            pltpu.VMEM((kv_local, 1, rows * group), F32),
            pltpu.VMEM((kv_local, 1, rows * group), F32),
            pltpu.VMEM((kv_local, rows * group, HD), F32),
            pltpu.VMEM((heads, rows), F32),
            pltpu.VMEM((heads, rows, rows), F32),
            pltpu.VMEM((GROUP, heads, HD), F32),
            pltpu.VMEM(state, BF16),
            pltpu.VMEM(state, BF16),
            pltpu.VMEM(state, BF16),
            pltpu.VMEM(state, BF16),
            pltpu.VMEM(state[1:], BF16),
            pltpu.VMEM(state[1:], BF16),
            pltpu.VMEM((rows, HD), F32),
            pltpu.VMEM((max(heads_dev - 1, 1), rows, HD), F32),
        ]
        + [dma((planes,))] * 10
        + [dma((GROUP - 1,))] * 4
        + [dma(((GROUP - 1) * PARTS,))] * 2
        + [dma((PARTS,))] * 2
        + [dma((max(heads_dev - 1, 1),))] * 2,
        compiler_params=pltpu.CompilerParams(
            collective_id=0, has_side_effects=True, vmem_limit_bytes=56 * 2**20
        ),
        name="mixers",
    )(lin_query, lin_key, lin_value, log_decay, norm_gain, attn_query,
      attn_key.transpose(1, 0, 2), attn_value.transpose(1, 0, 2))


def solution(mesh):
    planes = mesh.shape["ctx"] // GROUP
    return jax.shard_map(
        functools.partial(local, planes, mesh.shape["head"]),
        mesh=mesh,
        in_specs=(
            P("ctx", "head", None),
            P("ctx", "head", None),
            P("ctx", "head", None),
            P("head", "ctx"),
            P("head", None),
            P("ctx", "head", None),
            P("ctx", "head", None),
            P("ctx", "head", None),
        ),
        out_specs=(P("ctx", "head", None), P("ctx", "head", None)),
        check_vma=False,
    )
```

```python
import functools
import math

import jax
import jax.numpy as jnp
from jax import lax
from jax.experimental import pallas as pl
from jax.experimental.pallas import tpu as pltpu
from jax.sharding import PartitionSpec as P

QUERY_HEADS = 64
HD = 128
GROUP = 4
F32 = jnp.float32
BF16 = jnp.bfloat16
MESH = pl.DeviceIdType.MESH
NT = (((1,), (1,)), ((), ()))
TN = (((0,), (0,)), ((), ()))
MQ = 256
PARTS = 2


def silu(x):
    half = 0.5 * x
    return half + half * jnp.tanh(half)


def kernel(
    planes, heads_dev, lq, lk, lv, decay, gain, aq, k_in, v_in, lin_out, attn_out,
    qf, kf, vf, mixed, kv, qs, acc, m_ref, l_ref, ot, cum_ref, colb, lastb,
    sbuf, rs, prior, pr_send, carry, carry_out, rowsq, rowsq_in,
    z_s, z_r, zd_s, zd_r, x_s, x_r, y_s, y_r, dk_s, dk_r, dv_s, dv_r,
    s1_s, s1_r, la_s, la_r, s3_s, s3_r, c_s, c_r, h_s, h_r,
):
    rows, heads, _ = lq.shape
    kv_local = k_in.shape[0]
    group = heads // kv_local
    quarter = heads // GROUP
    me = lax.axis_index("ctx")
    my_head = lax.axis_index("head")
    z = me // GROUP
    p = me % GROUP
    base = z * GROUP
    px = jnp.where(p % 2 == 0, p + 1, p - 1)
    py = (p + 2) % GROUP
    pd = jnp.where(px >= 2, px - 2, px + 2)
    peers = (px, py, pd)
    has_up = z < planes - 1
    has_down = z > 0

    def remote(src, dst, s, r, ctx):
        return pltpu.make_async_remote_copy(
            src_ref=src, dst_ref=dst, send_sem=s, recv_sem=r,
            device_id={"ctx": ctx}, device_id_type=MESH,
        )

    kv[0, :, z, p] = k_in[...]
    kv[1, :, z, p] = v_in[...]

    barrier = pltpu.get_barrier_semaphore()
    for peer in peers:
        pl.semaphore_signal(barrier, inc=1, device_id={"ctx": base + peer}, device_id_type=MESH)
    for j in range(1, heads_dev):
        pl.semaphore_signal(
            barrier, inc=1, device_id={"head": (my_head + j) % heads_dev}, device_id_type=MESH
        )

    @pl.when(has_up)
    def _():
        pl.semaphore_signal(barrier, inc=1, device_id={"ctx": me + GROUP}, device_id_type=MESH)

    @pl.when(has_down)
    def _():
        pl.semaphore_signal(barrier, inc=1, device_id={"ctx": me - GROUP}, device_id_type=MESH)

    along = jnp.where(has_up, 1, 0) + jnp.where(has_down, 1, 0)
    pl.semaphore_wait(barrier, GROUP - 1 + heads_dev - 1 + along)

    def block(zz, col):
        return kv.at[:, :, zz, col]

    def up_copy(zz):
        return remote(block(zz, p), block(zz, p), z_s.at[zz], z_r.at[zz], me + GROUP)

    def up_diagonal(zz):
        return remote(block(zz, pd), block(zz, pd), zd_s.at[zz], zd_r.at[zz], me + GROUP)

    def x_copy(zz, col):
        return remote(block(zz, col), block(zz, col), x_s.at[zz], x_r.at[zz], base + px)

    def y_copy(zz, col):
        return remote(block(zz, col), block(zz, col), y_s.at[zz], y_r.at[zz], base + py)

    def dk_copy(col):
        return remote(kv.at[0, :, z, col], kv.at[0, :, z, col], dk_s, dk_r, base + py)

    def dv_copy(col):
        return remote(kv.at[1, :, z, col], kv.at[1, :, z, col], dv_s, dv_r, base + px)

    def send_column(zz):
        @pl.when(has_up)
        def _():
            up_copy(zz).start()

        x_copy(zz, p).start()
        y_copy(zz, p).start()

    send_column(z)

    step = 16

    def activate(src, dst):
        def body(i, _):
            t0 = pl.multiple_of(i * step, step)
            x = silu(src[pl.ds(t0, step)].astype(F32))
            r0 = pl.multiple_of(t0 * heads, step * heads)
            dst[pl.ds(r0, step * heads), :] = x.reshape(step * heads, HD)
            return 0

        lax.fori_loop(0, rows // step, body, 0)

    def head_rows(ref, h):
        return ref[pl.ds(h, rows, stride=heads), :]

    row_id = lax.broadcasted_iota(jnp.int32, (rows, rows), 0)
    col_id = lax.broadcasted_iota(jnp.int32, (rows, rows), 1)
    upper = jnp.where(row_id <= col_id, 1.0, 0.0).astype(F32)
    cum_all = lax.dot_general(
        decay[...], upper, (((1,), (0,)), ((), ())),
        precision=lax.Precision.HIGHEST, preferred_element_type=F32,
    )
    cum_ref[...] = cum_all
    lastb[p] = jnp.broadcast_to(cum_all[:, rows - 1 : rows], (heads, HD))
    last_copies = [
        remote(lastb.at[p], lastb.at[p], la_s.at[i], la_r.at[i], base + peer)
        for i, peer in enumerate(peers)
    ]
    for c in last_copies:
        c.start()

    activate(lk, kf)
    activate(lv, vf)

    together = min(4, quarter)

    def cum_row(h):
        return jnp.broadcast_to(cum_ref[pl.ds(h, 1), :], (rows, rows))

    def local_states(owner):
        def body(i, _):
            hs = [i * together + u for u in range(together)]
            ids = [owner * quarter + hh for hh in hs]
            ks = [head_rows(kf, h).astype(BF16).astype(F32) for h in ids]
            vs = [head_rows(vf, h).astype(BF16) for h in ids]
            lasts = [jnp.broadcast_to(lastb[p, pl.ds(h, 1), :], (rows, HD)) for h in ids]
            cols = [cum_row(h).T for h in ids]
            sks = [(k * jnp.exp(a - c)).astype(BF16) for k, a, c in zip(ks, lasts, cols)]
            sts = [
                lax.dot_general(sk, v, TN, preferred_element_type=F32) for sk, v in zip(sks, vs)
            ]
            for h, c in zip(ids, cols):
                colb[h] = c
            for hh, st in zip(hs, sts):
                sbuf[owner, hh] = st.astype(BF16)
            return 0

        lax.fori_loop(0, quarter // together, body, 0)

    s1 = [
        remote(sbuf.at[peer], rs.at[p], s1_s.at[i], s1_r.at[i], base + peer)
        for i, peer in enumerate(peers)
    ]
    for peer, c in zip(peers, s1):
        local_states(peer)
        c.start()
    local_states(p)

    def next_column(r):
        @pl.when(r <= z)
        def _():
            up_copy(z - r).wait_recv()
            send_column(z - r)

    x_copy(z, px).wait_recv()
    dk_copy(px).start()
    y_copy(z, py).wait_recv()
    dv_copy(py).start()
    next_column(1)

    def load_queries(i, _):
        t0 = pl.multiple_of(i * step, step)
        x = aq[pl.ds(t0, step)].astype(F32)
        for g in range(kv_local):
            part = x[:, g * group : (g + 1) * group, :].reshape(step * group, HD)
            r0 = pl.multiple_of(t0 * group, step * group)
            qs[g, pl.ds(r0, step * group), :] = part.astype(BF16)
        return 0

    lax.fori_loop(0, rows // step, load_queries, 0)
    activate(lq, qf)

    def inner(i, _):
        ids = [i * together + u for u in range(together)]
        qh = [head_rows(qf, h).astype(BF16) for h in ids]
        ks = [head_rows(kf, h).astype(BF16) for h in ids]
        vs = [head_rows(vf, h).astype(BF16) for h in ids]
        spread = [colb[h] - cum_row(h) for h in ids]
        sc = [lax.dot_general(q, k, NT, preferred_element_type=F32) for q, k in zip(qh, ks)]
        dm = [jnp.exp(jnp.where(row_id >= col_id, d, -1e30)) for d in spread]
        ws = [(a * d).astype(BF16) for a, d in zip(sc, dm)]
        outs = [jnp.dot(w, v, preferred_element_type=F32) for w, v in zip(ws, vs)]
        for h, o in zip(ids, outs):
            mixed[pl.ds(h, rows, stride=heads), :] = o
        return 0

    lax.fori_loop(0, heads // together, inner, 0)

    m_ref[...] = jnp.full(m_ref.shape, -1e30, F32)
    l_ref[...] = jnp.zeros(l_ref.shape, F32)
    acc[...] = jnp.zeros(acc.shape, F32)
    scale = HD ** (-0.5) * math.log2(math.e)
    span = GROUP * rows
    tiles = rows * group // MQ

    pair = 2
    sets = tiles // pair

    def attend(zz, masked):
        def body(i, _):
            g = i // sets
            starts = [pl.multiple_of(((i % sets) * pair + u) * MQ, MQ) for u in range(pair)]
            cols = [pl.ds(q0, MQ) for q0 in starts]
            k = kv[0, g, zz].reshape(span, HD)
            v = kv[1, g, zz].reshape(span, HD)
            ss = [
                lax.dot_general(k, qs[g, c, :], NT, preferred_element_type=F32) * scale
                for c in cols
            ]
            if masked:
                key_pos = lax.broadcasted_iota(jnp.int32, (span, MQ), 0)
                col_pos = lax.broadcasted_iota(jnp.int32, (span, MQ), 1)
                ss = [
                    jnp.where(key_pos <= p * rows + (q0 + col_pos) // group, x, -1e30)
                    for q0, x in zip(starts, ss)
                ]
            m_old = [m_ref[g, :, c] for c in cols]
            l_old = [l_ref[g, :, c] for c in cols]
            a_old = [acc[g, :, c] for c in cols]
            m_new = [
                jnp.maximum(m, jnp.max(x, axis=0, keepdims=True)) for m, x in zip(m_old, ss)
            ]
            alpha = [jnp.exp2(a - b) for a, b in zip(m_old, m_new)]
            es = [jnp.exp2(x - m) for x, m in zip(ss, m_new)]
            l_new = [
                old * a + jnp.sum(e, axis=0, keepdims=True)
                for old, a, e in zip(l_old, alpha, es)
            ]
            os = [
                lax.dot_general(v, e.astype(BF16), TN, preferred_element_type=F32) for e in es
            ]
            for u, c in enumerate(cols):
                m_ref[g, :, c] = m_new[u]
                l_ref[g, :, c] = l_new[u]
                acc[g, :, c] = a_old[u] * alpha[u] + os[u]
            return 0

        lax.fori_loop(0, kv_local * sets, body, 0)

    part = quarter // PARTS

    def carry_copy(j):
        own = pl.ds(j * part, part)
        return remote(carry_out.at[own], carry.at[own], c_s.at[j], c_r.at[j], me + GROUP)

    def prior_copy(j, i):
        own = pl.ds(j * part, part)
        n = j * (GROUP - 1) + i
        return remote(
            pr_send.at[peers[i], own], prior.at[p, own], s3_s.at[n], s3_r.at[n], base + peers[i]
        )

    def state_chain():
        for i in range(GROUP - 1):
            s1[i].wait_recv()
            last_copies[i].wait_recv()
        rs[p] = sbuf[p]

        @pl.when(jnp.logical_not(has_down))
        def _():
            carry[...] = jnp.zeros(carry.shape, BF16)

        for j in range(PARTS):

            @pl.when(has_down)
            def _():
                carry_copy(j).wait_recv()

            def one(n, _):
                hh = j * part + n
                h = p * quarter + hh
                state = carry[hh].astype(F32)
                for i in range(GROUP):
                    pr_send[i, hh] = state.astype(BF16)
                    d = jnp.exp(lastb[i, pl.ds(h, 1), :])
                    state = d * state + rs[i, hh].astype(F32)
                carry_out[hh] = state.astype(BF16)
                return 0

            lax.fori_loop(0, part, one, 0)

            @pl.when(has_up)
            def _():
                carry_copy(j).start()

            for i in range(GROUP - 1):
                prior_copy(j, i).start()
        prior[p] = pr_send[p]

    def turn(r, _):
        zz = z - r

        next_column(r + 2)

        @pl.when(r == 0)
        def _():
            dk_copy(pd).wait_recv()
            dv_copy(pd).wait_recv()

        @pl.when(r > 0)
        def _():
            x_copy(zz, px).wait_recv()
            y_copy(zz, py).wait_recv()
            up_diagonal(zz).wait_recv()

        @pl.when(has_up)
        def _():
            up_diagonal(zz).start()

        @pl.when(r == jnp.maximum(z - 1, 0))
        def _():
            state_chain()

        @pl.when(r == 0)
        def _():
            attend(zz, True)

        @pl.when(r > 0)
        def _():
            attend(zz, False)

        return 0

    lax.fori_loop(0, z + 1, turn, 0)

    for g in range(kv_local):
        for t in range(tiles):
            cols = slice(t * MQ, (t + 1) * MQ)
            ot[g, cols, :] = (acc[g, :, cols] / l_ref[g, :, cols]).T

    def store_attn(i, _):
        t0 = pl.multiple_of(i * step, step)
        r0 = pl.multiple_of(t0 * group, step * group)
        parts = [
            ot[g, pl.ds(r0, step * group), :].reshape(step, group, HD) for g in range(kv_local)
        ]
        attn_out[pl.ds(t0, step)] = jnp.concatenate(parts, axis=1).astype(BF16)
        return 0

    lax.fori_loop(0, rows // step, store_attn, 0)

    rowsq[...] = jnp.zeros(rowsq.shape, F32)

    def outer(owner, j):
        hs = [j * part + u for u in range(part)]
        ids = [owner * quarter + hh for hh in hs]
        qh = [head_rows(qf, h).astype(BF16) for h in ids]
        old = [head_rows(mixed, h) for h in ids]
        ps = [prior[owner, hh] for hh in hs]
        os = [jnp.dot(q, x, preferred_element_type=F32) for q, x in zip(qh, ps)]
        new = [a + o * jnp.exp(colb[h]) for a, o, h in zip(old, os, ids)]
        for h, x in zip(ids, new):
            mixed[pl.ds(h, rows, stride=heads), :] = x
        rowsq[...] += sum(x * x for x in new)

    for j in range(PARTS):
        outer(p, j)
        for i in range(GROUP - 1):
            prior_copy(j, i).wait_recv()
            outer(peers[i], j)
    h_copies = [
        pltpu.make_async_remote_copy(
            src_ref=rowsq, dst_ref=rowsq_in.at[j - 1], send_sem=h_s.at[j - 1],
            recv_sem=h_r.at[j - 1], device_id={"head": (my_head + j) % heads_dev},
            device_id_type=MESH,
        )
        for j in range(1, heads_dev)
    ]
    for c in h_copies:
        c.start()

    for c in h_copies:
        c.wait_recv()
    total = rowsq[...]
    for j in range(heads_dev - 1):
        total = total + rowsq_in[j]
    mean = jnp.sum(total, axis=1, keepdims=True) / (heads_dev * heads * HD)
    for c in h_copies:
        c.wait_send()
    rowsq[...] = jnp.broadcast_to(lax.rsqrt(mean + 1e-06), (rows, HD))

    def store_lin(i, _):
        t0 = pl.multiple_of(i * step, step)
        r0 = pl.multiple_of(t0 * heads, step * heads)
        x = mixed[pl.ds(r0, step * heads), :].reshape(step, heads, HD)
        inv = rowsq[pl.ds(t0, step), :].reshape(step, 1, HD)
        lin_out[pl.ds(t0, step)] = (x * inv * gain[...][None]).astype(BF16)
        return 0

    lax.fori_loop(0, rows // step, store_lin, 0)

    for c in last_copies + s1:
        c.wait_send()
    for j in range(PARTS):
        for i in range(GROUP - 1):
            prior_copy(j, i).wait_send()

    @pl.when(has_up)
    def _():
        for j in range(PARTS):
            carry_copy(j).wait_send()

    def drain(zz, _):
        @pl.when(has_up)
        def _():
            up_copy(zz).wait_send()
            up_diagonal(zz).wait_send()

        x_copy(zz, p).wait_send()
        y_copy(zz, p).wait_send()
        return 0

    lax.fori_loop(0, z + 1, drain, 0)
    dk_copy(px).wait_send()
    dv_copy(py).wait_send()


def local(planes, heads_dev, lin_query, lin_key, lin_value, log_decay, norm_gain,
          attn_query, attn_key, attn_value):
    rows, heads, _ = lin_query.shape
    kv_local = attn_key.shape[1]
    group = heads // kv_local
    quarter = heads // GROUP
    vmem = pl.BlockSpec(memory_space=pltpu.VMEM)
    dma = pltpu.SemaphoreType.DMA
    out = jax.ShapeDtypeStruct(lin_query.shape, BF16)
    state = (GROUP, quarter, HD, HD)
    return pl.pallas_call(
        functools.partial(kernel, planes, heads_dev),
        out_shape=(out, out),
        in_specs=[vmem] * 8,
        out_specs=(vmem, vmem),
        scratch_shapes=[
            pltpu.VMEM((rows * heads, HD), F32),
            pltpu.VMEM((rows * heads, HD), F32),
            pltpu.VMEM((rows * heads, HD), F32),
            pltpu.VMEM((rows * heads, HD), F32),
            pltpu.VMEM((2, kv_local, planes, GROUP, rows, HD), BF16),
            pltpu.VMEM((kv_local, rows * group, HD), BF16),
            pltpu.VMEM((kv_local, HD, rows * group), F32),
            pltpu.VMEM((kv_local, 1, rows * group), F32),
            pltpu.VMEM((kv_local, 1, rows * group), F32),
            pltpu.VMEM((kv_local, rows * group, HD), F32),
            pltpu.VMEM((heads, rows), F32),
            pltpu.VMEM((heads, rows, rows), F32),
            pltpu.VMEM((GROUP, heads, HD), F32),
            pltpu.VMEM(state, BF16),
            pltpu.VMEM(state, BF16),
            pltpu.VMEM(state, BF16),
            pltpu.VMEM(state, BF16),
            pltpu.VMEM(state[1:], BF16),
            pltpu.VMEM(state[1:], BF16),
            pltpu.VMEM((rows, HD), F32),
            pltpu.VMEM((max(heads_dev - 1, 1), rows, HD), F32),
        ]
        + [dma((planes,))] * 8
        + [dma] * 4
        + [dma((GROUP - 1,))] * 4
        + [dma(((GROUP - 1) * PARTS,))] * 2
        + [dma((PARTS,))] * 2
        + [dma((max(heads_dev - 1, 1),))] * 2,
        compiler_params=pltpu.CompilerParams(
            collective_id=0, has_side_effects=True, vmem_limit_bytes=56 * 2**20
        ),
        name="mixers",
    )(lin_query, lin_key, lin_value, log_decay, norm_gain, attn_query,
      attn_key.transpose(1, 0, 2), attn_value.transpose(1, 0, 2))


def solution(mesh):
    planes = mesh.shape["ctx"] // GROUP
    return jax.shard_map(
        functools.partial(local, planes, mesh.shape["head"]),
        mesh=mesh,
        in_specs=(
            P("ctx", "head", None),
            P("ctx", "head", None),
            P("ctx", "head", None),
            P("head", "ctx"),
            P("head", None),
            P("ctx", "head", None),
            P("ctx", "head", None),
            P("ctx", "head", None),
        ),
        out_specs=(P("ctx", "head", None), P("ctx", "head", None)),
        check_vma=False,
    )
```

```python
import functools
import math

import jax
import jax.numpy as jnp
from jax import lax
from jax.experimental import pallas as pl
from jax.experimental.pallas import tpu as pltpu
from jax.sharding import PartitionSpec as P

QUERY_HEADS = 64
HD = 128
GROUP = 4
F32 = jnp.float32
BF16 = jnp.bfloat16
MESH = pl.DeviceIdType.MESH
NT = (((1,), (1,)), ((), ()))
TN = (((0,), (0,)), ((), ()))
MQ = 256
PARTS = 2


def silu(x):
    half = 0.5 * x
    return half + half * jnp.tanh(half)


def kernel(
    planes, heads_dev, lq_in, lk_in, lv_in, decay, gain, aq_in, k_in, v_in, lin_hbm, attn_hbm,
    lq, lk, lv, aq, lin_out, attn_out, in_sem, out_sem,
    qf, kf, vf, mixed, kv, qs, acc, m_ref, l_ref, ot, cum_ref, colb, lastb,
    sbuf, rs, prior, pr_send, carry, carry_out, rowsq, rowsq_in,
    z_s, z_r, zd_s, zd_r, x_s, x_r, y_s, y_r, dk_s, dk_r, dv_s, dv_r,
    s1_s, s1_r, la_s, la_r, s3_s, s3_r, c_s, c_r, h_s, h_r,
):
    loads = [
        pltpu.make_async_copy(src, dst, in_sem.at[i])
        for i, (src, dst) in enumerate(((lk_in, lk), (lv_in, lv), (aq_in, aq), (lq_in, lq)))
    ]
    for c in loads:
        c.start()
    rows, heads, _ = lq.shape
    kv_local = k_in.shape[0]
    group = heads // kv_local
    quarter = heads // GROUP
    me = lax.axis_index("ctx")
    my_head = lax.axis_index("head")
    z = me // GROUP
    p = me % GROUP
    base = z * GROUP
    px = jnp.where(p % 2 == 0, p + 1, p - 1)
    py = (p + 2) % GROUP
    pd = jnp.where(px >= 2, px - 2, px + 2)
    peers = (px, py, pd)
    has_up = z < planes - 1
    has_down = z > 0

    def remote(src, dst, s, r, ctx):
        return pltpu.make_async_remote_copy(
            src_ref=src, dst_ref=dst, send_sem=s, recv_sem=r,
            device_id={"ctx": ctx}, device_id_type=MESH,
        )

    kv[0, :, z, p] = k_in[...]
    kv[1, :, z, p] = v_in[...]

    barrier = pltpu.get_barrier_semaphore()
    for peer in peers:
        pl.semaphore_signal(barrier, inc=1, device_id={"ctx": base + peer}, device_id_type=MESH)
    for j in range(1, heads_dev):
        pl.semaphore_signal(
            barrier, inc=1, device_id={"head": (my_head + j) % heads_dev}, device_id_type=MESH
        )

    @pl.when(has_up)
    def _():
        pl.semaphore_signal(barrier, inc=1, device_id={"ctx": me + GROUP}, device_id_type=MESH)

    @pl.when(has_down)
    def _():
        pl.semaphore_signal(barrier, inc=1, device_id={"ctx": me - GROUP}, device_id_type=MESH)

    along = jnp.where(has_up, 1, 0) + jnp.where(has_down, 1, 0)
    pl.semaphore_wait(barrier, GROUP - 1 + heads_dev - 1 + along)

    def block(zz, col):
        return kv.at[:, :, zz, col]

    def up_copy(zz):
        return remote(block(zz, p), block(zz, p), z_s.at[zz], z_r.at[zz], me + GROUP)

    def up_diagonal(zz):
        return remote(block(zz, pd), block(zz, pd), zd_s.at[zz], zd_r.at[zz], me + GROUP)

    def x_copy(zz, col):
        return remote(block(zz, col), block(zz, col), x_s.at[zz], x_r.at[zz], base + px)

    def y_copy(zz, col):
        return remote(block(zz, col), block(zz, col), y_s.at[zz], y_r.at[zz], base + py)

    def dk_copy(col):
        return remote(kv.at[0, :, z, col], kv.at[0, :, z, col], dk_s, dk_r, base + py)

    def dv_copy(col):
        return remote(kv.at[1, :, z, col], kv.at[1, :, z, col], dv_s, dv_r, base + px)

    def send_in_plane(zz):
        x_copy(zz, p).start()
        y_copy(zz, p).start()

    def send_up(zz):
        @pl.when(has_up)
        def _():
            up_copy(zz).start()

    send_in_plane(z)
    send_up(z)

    step = 16

    def activate(src, dst):
        def body(i, _):
            t0 = pl.multiple_of(i * step, step)
            x = silu(src[pl.ds(t0, step)].astype(F32))
            r0 = pl.multiple_of(t0 * heads, step * heads)
            dst[pl.ds(r0, step * heads), :] = x.reshape(step * heads, HD)
            return 0

        lax.fori_loop(0, rows // step, body, 0)

    def head_rows(ref, h):
        return ref[pl.ds(h, rows, stride=heads), :]

    row_id = lax.broadcasted_iota(jnp.int32, (rows, rows), 0)
    col_id = lax.broadcasted_iota(jnp.int32, (rows, rows), 1)
    upper = jnp.where(row_id <= col_id, 1.0, 0.0).astype(F32)
    cum_all = lax.dot_general(
        decay[...], upper, (((1,), (0,)), ((), ())),
        precision=lax.Precision.HIGHEST, preferred_element_type=F32,
    )
    cum_ref[...] = cum_all
    lastb[p] = jnp.broadcast_to(cum_all[:, rows - 1 : rows], (heads, HD))
    last_copies = [
        remote(lastb.at[p], lastb.at[p], la_s.at[i], la_r.at[i], base + peer)
        for i, peer in enumerate(peers)
    ]
    for c in last_copies:
        c.start()

    loads[0].wait()
    activate(lk, kf)
    loads[1].wait()
    activate(lv, vf)

    together = min(4, quarter)

    def cum_row(h):
        return jnp.broadcast_to(cum_ref[pl.ds(h, 1), :], (rows, rows))

    def local_states(owner):
        def body(i, _):
            hs = [i * together + u for u in range(together)]
            ids = [owner * quarter + hh for hh in hs]
            ks = [head_rows(kf, h).astype(BF16).astype(F32) for h in ids]
            vs = [head_rows(vf, h).astype(BF16) for h in ids]
            lasts = [jnp.broadcast_to(lastb[p, pl.ds(h, 1), :], (rows, HD)) for h in ids]
            cols = [cum_row(h).T for h in ids]
            sks = [(k * jnp.exp(a - c)).astype(BF16) for k, a, c in zip(ks, lasts, cols)]
            sts = [
                lax.dot_general(sk, v, TN, preferred_element_type=F32) for sk, v in zip(sks, vs)
            ]
            for h, c in zip(ids, cols):
                colb[h] = c
            for hh, st in zip(hs, sts):
                sbuf[owner, hh] = st.astype(BF16)
            return 0

        lax.fori_loop(0, quarter // together, body, 0)

    s1 = [
        remote(sbuf.at[peer], rs.at[p], s1_s.at[i], s1_r.at[i], base + peer)
        for i, peer in enumerate(peers)
    ]
    for peer, c in zip(peers, s1):
        local_states(peer)
        c.start()
    local_states(p)

    def next_column(r):
        @pl.when(r <= z)
        def _():
            up_copy(z - r).wait_recv()
            send_up(z - r)

    x_copy(z, px).wait_recv()
    dk_copy(px).start()
    y_copy(z, py).wait_recv()
    dv_copy(py).start()
    next_column(1)

    def load_queries(i, _):
        t0 = pl.multiple_of(i * step, step)
        x = aq[pl.ds(t0, step)].astype(F32)
        for g in range(kv_local):
            part = x[:, g * group : (g + 1) * group, :].reshape(step * group, HD)
            r0 = pl.multiple_of(t0 * group, step * group)
            qs[g, pl.ds(r0, step * group), :] = part.astype(BF16)
        return 0

    loads[2].wait()
    lax.fori_loop(0, rows // step, load_queries, 0)
    loads[3].wait()
    activate(lq, qf)

    def inner(i, _):
        ids = [i * together + u for u in range(together)]
        qh = [head_rows(qf, h).astype(BF16) for h in ids]
        ks = [head_rows(kf, h).astype(BF16) for h in ids]
        vs = [head_rows(vf, h).astype(BF16) for h in ids]
        spread = [colb[h] - cum_row(h) for h in ids]
        sc = [lax.dot_general(q, k, NT, preferred_element_type=F32) for q, k in zip(qh, ks)]
        dm = [jnp.exp(jnp.where(row_id >= col_id, d, -1e30)) for d in spread]
        ws = [(a * d).astype(BF16) for a, d in zip(sc, dm)]
        outs = [jnp.dot(w, v, preferred_element_type=F32) for w, v in zip(ws, vs)]
        for h, o in zip(ids, outs):
            mixed[pl.ds(h, rows, stride=heads), :] = o
        return 0

    lax.fori_loop(0, heads // together, inner, 0)

    m_ref[...] = jnp.full(m_ref.shape, -1e30, F32)
    l_ref[...] = jnp.zeros(l_ref.shape, F32)
    acc[...] = jnp.zeros(acc.shape, F32)
    scale = HD ** (-0.5) * math.log2(math.e)
    span = GROUP * rows
    tiles = rows * group // MQ

    pair = 2
    sets = tiles // pair

    def attend(zz, masked):
        def body(i, _):
            g = i // sets
            starts = [pl.multiple_of(((i % sets) * pair + u) * MQ, MQ) for u in range(pair)]
            cols = [pl.ds(q0, MQ) for q0 in starts]
            k = kv[0, g, zz].reshape(span, HD)
            v = kv[1, g, zz].reshape(span, HD)
            ss = [
                lax.dot_general(k, qs[g, c, :], NT, preferred_element_type=F32) * scale
                for c in cols
            ]
            if masked:
                key_pos = lax.broadcasted_iota(jnp.int32, (span, MQ), 0)
                col_pos = lax.broadcasted_iota(jnp.int32, (1, MQ), 1)
                ss = [
                    jnp.where(key_pos <= p * rows + (q0 + col_pos) // group, x, -1e30)
                    for q0, x in zip(starts, ss)
                ]
            m_old = [m_ref[g, :, c] for c in cols]
            l_old = [l_ref[g, :, c] for c in cols]
            a_old = [acc[g, :, c] for c in cols]
            m_new = [
                jnp.maximum(m, jnp.max(x, axis=0, keepdims=True)) for m, x in zip(m_old, ss)
            ]
            alpha = [jnp.exp2(a - b) for a, b in zip(m_old, m_new)]
            es = [jnp.exp2(x - m) for x, m in zip(ss, m_new)]
            l_new = [
                old * a + jnp.sum(e, axis=0, keepdims=True)
                for old, a, e in zip(l_old, alpha, es)
            ]
            os = [
                lax.dot_general(v, e.astype(BF16), TN, preferred_element_type=F32) for e in es
            ]
            for u, c in enumerate(cols):
                m_ref[g, :, c] = m_new[u]
                l_ref[g, :, c] = l_new[u]
                acc[g, :, c] = a_old[u] * alpha[u] + os[u]
            return 0

        lax.fori_loop(0, kv_local * sets, body, 0)

    part = quarter // PARTS

    sub = 2 if part % 2 == 0 else 1
    piece = part // sub

    def carry_copy(n):
        own = pl.ds(n * piece, piece)
        return remote(carry_out.at[own], carry.at[own], c_s.at[n], c_r.at[n], me + GROUP)

    def prior_copy(j, i):
        own = pl.ds(j * part, part)
        n = j * (GROUP - 1) + i
        return remote(
            pr_send.at[peers[i], own], prior.at[p, own], s3_s.at[n], s3_r.at[n], base + peers[i]
        )

    def state_chain():
        for i in range(GROUP - 1):
            s1[i].wait_recv()
            last_copies[i].wait_recv()
        rs[p] = sbuf[p]

        @pl.when(jnp.logical_not(has_down))
        def _():
            carry[...] = jnp.zeros(carry.shape, BF16)

        for n in range(PARTS * sub):

            @pl.when(has_down)
            def _():
                carry_copy(n).wait_recv()

            for hh in range(n * piece, (n + 1) * piece):
                h = p * quarter + hh
                state = carry[hh].astype(F32)
                for i in range(GROUP):
                    pr_send[i, hh] = state.astype(BF16)
                    d = jnp.exp(lastb[i, pl.ds(h, 1), :])
                    state = d * state + rs[i, hh].astype(F32)
                carry_out[hh] = state.astype(BF16)

            @pl.when(has_up)
            def _():
                carry_copy(n).start()

            if n % sub == sub - 1:
                for i in range(GROUP - 1):
                    prior_copy(n // sub, i).start()
        prior[p] = pr_send[p]

    def turn(r, _):
        zz = z - r

        @pl.when(r < z)
        def _():
            send_in_plane(zz - 1)

        next_column(r + 2)

        @pl.when(r == 0)
        def _():
            dk_copy(pd).wait_recv()
            dv_copy(pd).wait_recv()

        @pl.when(r > 0)
        def _():
            x_copy(zz, px).wait_recv()
            y_copy(zz, py).wait_recv()
            up_diagonal(zz).wait_recv()

        @pl.when(has_up)
        def _():
            up_diagonal(zz).start()

        @pl.when(r == z)
        def _():
            state_chain()

        @pl.when(r == 0)
        def _():
            attend(zz, True)

        @pl.when(r > 0)
        def _():
            attend(zz, False)

        return 0

    lax.fori_loop(0, z + 1, turn, 0)

    for g in range(kv_local):
        for t in range(tiles):
            cols = slice(t * MQ, (t + 1) * MQ)
            ot[g, cols, :] = (acc[g, :, cols] / l_ref[g, :, cols]).T

    rowsq[...] = jnp.zeros(rowsq.shape, F32)

    def outer(owner, j):
        hs = [j * part + u for u in range(part)]
        ids = [owner * quarter + hh for hh in hs]
        qh = [head_rows(qf, h).astype(BF16) for h in ids]
        old = [head_rows(mixed, h) for h in ids]
        ps = [prior[owner, hh] for hh in hs]
        os = [jnp.dot(q, x, preferred_element_type=F32) for q, x in zip(qh, ps)]
        new = [a + o * jnp.exp(colb[h]) for a, o, h in zip(old, os, ids)]
        for h, x in zip(ids, new):
            mixed[pl.ds(h, rows, stride=heads), :] = x
        rowsq[...] += sum(x * x for x in new)

    for j in range(PARTS):
        outer(p, j)
        for i in range(GROUP - 1):
            prior_copy(j, i).wait_recv()
            outer(peers[i], j)
    h_copies = [
        pltpu.make_async_remote_copy(
            src_ref=rowsq, dst_ref=rowsq_in.at[j - 1], send_sem=h_s.at[j - 1],
            recv_sem=h_r.at[j - 1], device_id={"head": (my_head + j) % heads_dev},
            device_id_type=MESH,
        )
        for j in range(1, heads_dev)
    ]
    for c in h_copies:
        c.start()

    def store_attn(i, _):
        t0 = pl.multiple_of(i * step, step)
        r0 = pl.multiple_of(t0 * group, step * group)
        parts = [
            ot[g, pl.ds(r0, step * group), :].reshape(step, group, HD) for g in range(kv_local)
        ]
        attn_out[pl.ds(t0, step)] = jnp.concatenate(parts, axis=1).astype(BF16)
        return 0

    lax.fori_loop(0, rows // step, store_attn, 0)
    attn_store = pltpu.make_async_copy(attn_out, attn_hbm, out_sem.at[0])
    attn_store.start()

    for c in h_copies:
        c.wait_recv()
    total = rowsq[...]
    for j in range(heads_dev - 1):
        total = total + rowsq_in[j]
    mean = jnp.sum(total, axis=1, keepdims=True) / (heads_dev * heads * HD)
    for c in h_copies:
        c.wait_send()
    rowsq[...] = jnp.broadcast_to(lax.rsqrt(mean + 1e-06), (rows, HD))

    def store_lin(i, _):
        t0 = pl.multiple_of(i * step, step)
        r0 = pl.multiple_of(t0 * heads, step * heads)
        x = mixed[pl.ds(r0, step * heads), :].reshape(step, heads, HD)
        inv = rowsq[pl.ds(t0, step), :].reshape(step, 1, HD)
        lin_out[pl.ds(t0, step)] = (x * inv * gain[...][None]).astype(BF16)
        return 0

    halves = 2
    lin_stores = []
    for j in range(halves):
        n = rows // step // halves
        lax.fori_loop(j * n, (j + 1) * n, store_lin, 0)
        own = pl.ds(j * n * step, n * step)
        lin_stores.append(
            pltpu.make_async_copy(lin_out.at[own], lin_hbm.at[own], out_sem.at[1 + j])
        )
        lin_stores[j].start()

    for c in last_copies + s1:
        c.wait_send()
    for j in range(PARTS):
        for i in range(GROUP - 1):
            prior_copy(j, i).wait_send()

    @pl.when(has_up)
    def _():
        for n in range(PARTS * sub):
            carry_copy(n).wait_send()

    def drain(zz, _):
        @pl.when(has_up)
        def _():
            up_copy(zz).wait_send()
            up_diagonal(zz).wait_send()

        x_copy(zz, p).wait_send()
        y_copy(zz, p).wait_send()
        return 0

    lax.fori_loop(0, z + 1, drain, 0)
    dk_copy(px).wait_send()
    dv_copy(py).wait_send()
    attn_store.wait()
    for c in lin_stores:
        c.wait()


def local(planes, heads_dev, lin_query, lin_key, lin_value, log_decay, norm_gain,
          attn_query, attn_key, attn_value):
    rows, heads, _ = lin_query.shape
    kv_local = attn_key.shape[1]
    group = heads // kv_local
    quarter = heads // GROUP
    vmem = pl.BlockSpec(memory_space=pltpu.VMEM)
    hbm = pl.BlockSpec(memory_space=pl.ANY)
    dma = pltpu.SemaphoreType.DMA
    out = jax.ShapeDtypeStruct(lin_query.shape, BF16)
    state = (GROUP, quarter, HD, HD)
    return pl.pallas_call(
        functools.partial(kernel, planes, heads_dev),
        out_shape=(out, out),
        in_specs=[hbm, hbm, hbm, vmem, vmem, hbm, vmem, vmem],
        out_specs=(hbm, hbm),
        scratch_shapes=[pltpu.VMEM(lin_query.shape, BF16)] * 6
        + [dma((4,)), dma((3,))]
        + [
            pltpu.VMEM((rows * heads, HD), F32),
            pltpu.VMEM((rows * heads, HD), F32),
            pltpu.VMEM((rows * heads, HD), F32),
            pltpu.VMEM((rows * heads, HD), F32),
            pltpu.VMEM((2, kv_local, planes, GROUP, rows, HD), BF16),
            pltpu.VMEM((kv_local, rows * group, HD), BF16),
            pltpu.VMEM((kv_local, HD, rows * group), F32),
            pltpu.VMEM((kv_local, 1, rows * group), F32),
            pltpu.VMEM((kv_local, 1, rows * group), F32),
            pltpu.VMEM((kv_local, rows * group, HD), F32),
            pltpu.VMEM((heads, rows), F32),
            pltpu.VMEM((heads, rows, rows), F32),
            pltpu.VMEM((GROUP, heads, HD), F32),
            pltpu.VMEM(state, BF16),
            pltpu.VMEM(state, BF16),
            pltpu.VMEM(state, BF16),
            pltpu.VMEM(state, BF16),
            pltpu.VMEM(state[1:], BF16),
            pltpu.VMEM(state[1:], BF16),
            pltpu.VMEM((rows, HD), F32),
            pltpu.VMEM((max(heads_dev - 1, 1), rows, HD), F32),
        ]
        + [dma((planes,))] * 8
        + [dma] * 4
        + [dma((GROUP - 1,))] * 4
        + [dma(((GROUP - 1) * PARTS,))] * 2
        + [dma((quarter,))] * 2
        + [dma((max(heads_dev - 1, 1),))] * 2,
        compiler_params=pltpu.CompilerParams(
            collective_id=0, has_side_effects=True, vmem_limit_bytes=56 * 2**20
        ),
        name="mixers",
    )(lin_query, lin_key, lin_value, log_decay, norm_gain, attn_query,
      attn_key.transpose(1, 0, 2), attn_value.transpose(1, 0, 2))


def solution(mesh):
    planes = mesh.shape["ctx"] // GROUP
    return jax.shard_map(
        functools.partial(local, planes, mesh.shape["head"]),
        mesh=mesh,
        in_specs=(
            P("ctx", "head", None),
            P("ctx", "head", None),
            P("ctx", "head", None),
            P("head", "ctx"),
            P("head", None),
            P("ctx", "head", None),
            P("ctx", "head", None),
            P("ctx", "head", None),
        ),
        out_specs=(P("ctx", "head", None), P("ctx", "head", None)),
        check_vma=False,
    )
```

```python
import functools
import math

import jax
import jax.numpy as jnp
from jax import lax
from jax.experimental import pallas as pl
from jax.experimental.pallas import tpu as pltpu
from jax.sharding import PartitionSpec as P

QUERY_HEADS = 64
HD = 128
GROUP = 4
F32 = jnp.float32
BF16 = jnp.bfloat16
MESH = pl.DeviceIdType.MESH
NT = (((1,), (1,)), ((), ()))
TN = (((0,), (0,)), ((), ()))
MQ = 256
PARTS = 2


def silu(x):
    half = 0.5 * x
    return half + half * jnp.tanh(half)


def kernel(
    planes, heads_dev, lq_in, lk_in, lv_in, decay, gain, aq_in, k_in, v_in, lin_hbm, attn_hbm,
    lq, lk, lv, aq, lin_out, attn_out, in_sem, out_sem, by_row,
    qf, kf, vf, mixed, kv, qs, acc, m_ref, l_ref, ot, cum_ref, colb, lastb,
    sbuf, rs, prior, pr_send, carry, carry_out, rowsq, rowsq_in,
    z_s, z_r, zd_s, zd_r, x_s, x_r, y_s, y_r, dk_s, dk_r, dv_s, dv_r,
    s1_s, s1_r, la_s, la_r, s3_s, s3_r, c_s, c_r, h_s, h_r,
):
    loads = [
        pltpu.make_async_copy(src, dst, in_sem.at[i])
        for i, (src, dst) in enumerate(((lk_in, lk), (lv_in, lv), (aq_in, aq), (lq_in, lq)))
    ]
    for c in loads:
        c.start()
    rows, heads, _ = lq.shape
    kv_local = k_in.shape[1]
    group = heads // kv_local
    quarter = heads // GROUP
    me = lax.axis_index("ctx")
    my_head = lax.axis_index("head")
    z = me // GROUP
    p = me % GROUP
    base = z * GROUP
    px = jnp.where(p % 2 == 0, p + 1, p - 1)
    py = (p + 2) % GROUP
    pd = jnp.where(px >= 2, px - 2, px + 2)
    peers = (px, py, pd)
    has_up = z < planes - 1
    has_down = z > 0

    def remote(src, dst, s, r, ctx):
        return pltpu.make_async_remote_copy(
            src_ref=src, dst_ref=dst, send_sem=s, recv_sem=r,
            device_id={"ctx": ctx}, device_id_type=MESH,
        )

    slots = -(-2 * kv_local // 8) * 8
    both = [k_in[...].astype(F32), v_in[...].astype(F32)]
    if slots > 2 * kv_local:
        both.append(jnp.zeros((rows, slots - 2 * kv_local, HD), F32))
    by_row[...] = jnp.concatenate(both, axis=1).reshape(rows * slots, HD)
    for j in range(2):
        for g in range(kv_local):
            kv[j, g, z, p] = by_row[pl.ds(j * kv_local + g, rows, stride=slots), :].astype(BF16)

    barrier = pltpu.get_barrier_semaphore()
    for peer in peers:
        pl.semaphore_signal(barrier, inc=1, device_id={"ctx": base + peer}, device_id_type=MESH)
    for j in range(1, heads_dev):
        pl.semaphore_signal(
            barrier, inc=1, device_id={"head": (my_head + j) % heads_dev}, device_id_type=MESH
        )

    @pl.when(has_up)
    def _():
        pl.semaphore_signal(barrier, inc=1, device_id={"ctx": me + GROUP}, device_id_type=MESH)

    @pl.when(has_down)
    def _():
        pl.semaphore_signal(barrier, inc=1, device_id={"ctx": me - GROUP}, device_id_type=MESH)

    along = jnp.where(has_up, 1, 0) + jnp.where(has_down, 1, 0)
    pl.semaphore_wait(barrier, GROUP - 1 + heads_dev - 1 + along)

    def block(zz, col):
        return kv.at[:, :, zz, col]

    def up_copy(zz):
        return remote(block(zz, p), block(zz, p), z_s.at[zz], z_r.at[zz], me + GROUP)

    def up_diagonal(zz):
        return remote(block(zz, pd), block(zz, pd), zd_s.at[zz], zd_r.at[zz], me + GROUP)

    def x_copy(zz, col):
        return remote(block(zz, col), block(zz, col), x_s.at[zz], x_r.at[zz], base + px)

    def y_copy(zz, col):
        return remote(block(zz, col), block(zz, col), y_s.at[zz], y_r.at[zz], base + py)

    def dk_copy(col):
        return remote(kv.at[0, :, z, col], kv.at[0, :, z, col], dk_s, dk_r, base + py)

    def dv_copy(col):
        return remote(kv.at[1, :, z, col], kv.at[1, :, z, col], dv_s, dv_r, base + px)

    def send_in_plane(zz):
        x_copy(zz, p).start()
        y_copy(zz, p).start()

    def send_up(zz):
        @pl.when(has_up)
        def _():
            up_copy(zz).start()

    send_in_plane(z)
    send_up(z)

    step = 16

    def activate(src, dst):
        def body(i, _):
            t0 = pl.multiple_of(i * step, step)
            x = silu(src[pl.ds(t0, step)].astype(F32))
            r0 = pl.multiple_of(t0 * heads, step * heads)
            dst[pl.ds(r0, step * heads), :] = x.reshape(step * heads, HD)
            return 0

        lax.fori_loop(0, rows // step, body, 0)

    def head_rows(ref, h):
        return ref[pl.ds(h, rows, stride=heads), :]

    row_id = lax.broadcasted_iota(jnp.int32, (rows, rows), 0)
    col_id = lax.broadcasted_iota(jnp.int32, (rows, rows), 1)
    upper = jnp.where(row_id <= col_id, 1.0, 0.0).astype(F32)
    cum_all = lax.dot_general(
        decay[...], upper, (((1,), (0,)), ((), ())),
        precision=lax.Precision.HIGHEST, preferred_element_type=F32,
    )
    cum_ref[...] = cum_all
    lastb[p] = jnp.broadcast_to(cum_all[:, rows - 1 : rows], (heads, HD))
    last_copies = [
        remote(lastb.at[p], lastb.at[p], la_s.at[i], la_r.at[i], base + peer)
        for i, peer in enumerate(peers)
    ]
    for c in last_copies:
        c.start()

    loads[0].wait()
    activate(lk, kf)
    loads[1].wait()
    activate(lv, vf)

    together = min(4, quarter)

    def cum_row(h):
        return jnp.broadcast_to(cum_ref[pl.ds(h, 1), :], (rows, rows))

    def local_states(owner):
        def body(i, _):
            hs = [i * together + u for u in range(together)]
            ids = [owner * quarter + hh for hh in hs]
            ks = [head_rows(kf, h).astype(BF16).astype(F32) for h in ids]
            vs = [head_rows(vf, h).astype(BF16) for h in ids]
            lasts = [jnp.broadcast_to(lastb[p, pl.ds(h, 1), :], (rows, HD)) for h in ids]
            cols = [cum_row(h).T for h in ids]
            sks = [(k * jnp.exp(a - c)).astype(BF16) for k, a, c in zip(ks, lasts, cols)]
            sts = [
                lax.dot_general(sk, v, TN, preferred_element_type=F32) for sk, v in zip(sks, vs)
            ]
            for h, c in zip(ids, cols):
                colb[h] = c
            for hh, st in zip(hs, sts):
                sbuf[owner, hh] = st.astype(BF16)
            return 0

        lax.fori_loop(0, quarter // together, body, 0)

    s1 = [
        remote(sbuf.at[peer], rs.at[p], s1_s.at[i], s1_r.at[i], base + peer)
        for i, peer in enumerate(peers)
    ]
    for peer, c in zip(peers, s1):
        local_states(peer)
        c.start()
    local_states(p)

    def next_column(r):
        @pl.when(r <= z)
        def _():
            up_copy(z - r).wait_recv()
            send_up(z - r)

    x_copy(z, px).wait_recv()
    dk_copy(px).start()
    y_copy(z, py).wait_recv()
    dv_copy(py).start()
    next_column(1)

    def load_queries(i, _):
        t0 = pl.multiple_of(i * step, step)
        x = aq[pl.ds(t0, step)].astype(F32)
        for g in range(kv_local):
            part = x[:, g * group : (g + 1) * group, :].reshape(step * group, HD)
            r0 = pl.multiple_of(t0 * group, step * group)
            qs[g, pl.ds(r0, step * group), :] = part.astype(BF16)
        return 0

    loads[2].wait()
    lax.fori_loop(0, rows // step, load_queries, 0)
    loads[3].wait()
    activate(lq, qf)

    def inner(i, _):
        ids = [i * together + u for u in range(together)]
        qh = [head_rows(qf, h).astype(BF16) for h in ids]
        ks = [head_rows(kf, h).astype(BF16) for h in ids]
        vs = [head_rows(vf, h).astype(BF16) for h in ids]
        spread = [colb[h] - cum_row(h) for h in ids]
        sc = [lax.dot_general(q, k, NT, preferred_element_type=F32) for q, k in zip(qh, ks)]
        dm = [jnp.exp(jnp.where(row_id >= col_id, d, -1e30)) for d in spread]
        ws = [(a * d).astype(BF16) for a, d in zip(sc, dm)]
        outs = [jnp.dot(w, v, preferred_element_type=F32) for w, v in zip(ws, vs)]
        for h, o in zip(ids, outs):
            mixed[pl.ds(h, rows, stride=heads), :] = o
        return 0

    lax.fori_loop(0, heads // together, inner, 0)

    m_ref[...] = jnp.full(m_ref.shape, -1e30, F32)
    l_ref[...] = jnp.zeros(l_ref.shape, F32)
    acc[...] = jnp.zeros(acc.shape, F32)
    scale = HD ** (-0.5) * math.log2(math.e)
    span = GROUP * rows
    tiles = rows * group // MQ

    def attend(zz, masked):
        def body(g, _):
            cols = [pl.ds(t * MQ, MQ) for t in range(tiles)]
            k = kv[0, g, zz].reshape(span, HD)
            v = kv[1, g, zz].reshape(span, HD)
            m_old = [m_ref[g, :, c] for c in cols]
            l_old = [l_ref[g, :, c] for c in cols]

            def scores(t):
                s = lax.dot_general(k, qs[g, cols[t], :], NT, preferred_element_type=F32) * scale
                if masked:
                    key_pos = lax.broadcasted_iota(jnp.int32, (span, MQ), 0)
                    col_pos = lax.broadcasted_iota(jnp.int32, (1, MQ), 1)
                    s = jnp.where(key_pos <= p * rows + (t * MQ + col_pos) // group, s, -1e30)
                return s

            def probs(t, s):
                m_new = jnp.maximum(m_old[t], jnp.max(s, axis=0, keepdims=True))
                alpha = jnp.exp2(m_old[t] - m_new)
                e = jnp.exp2(s - m_new)
                m_ref[g, :, cols[t]] = m_new
                l_ref[g, :, cols[t]] = l_old[t] * alpha + jnp.sum(e, axis=0, keepdims=True)
                return e.astype(BF16), alpha

            def values(t, e, alpha):
                o = lax.dot_general(v, e, TN, preferred_element_type=F32)
                acc[g, :, cols[t]] = acc[g, :, cols[t]] * alpha + o

            ss, es = {}, {}
            for t in range(tiles + 2):
                if t < tiles:
                    ss[t] = scores(t)
                if 0 <= t - 2 < tiles:
                    values(t - 2, *es.pop(t - 2))
                if 0 <= t - 1 < tiles:
                    es[t - 1] = probs(t - 1, ss.pop(t - 1))
            return 0

        lax.fori_loop(0, kv_local, body, 0)

    part = quarter // PARTS

    sub = 2 if part % 2 == 0 else 1
    piece = part // sub

    def carry_copy(n):
        own = pl.ds(n * piece, piece)
        return remote(carry_out.at[own], carry.at[own], c_s.at[n], c_r.at[n], me + GROUP)

    def prior_copy(j, i):
        own = pl.ds(j * part, part)
        n = j * (GROUP - 1) + i
        return remote(
            pr_send.at[peers[i], own], prior.at[p, own], s3_s.at[n], s3_r.at[n], base + peers[i]
        )

    def state_chain():
        for i in range(GROUP - 1):
            s1[i].wait_recv()
            last_copies[i].wait_recv()
        rs[p] = sbuf[p]

        @pl.when(jnp.logical_not(has_down))
        def _():
            carry[...] = jnp.zeros(carry.shape, BF16)

        for n in range(PARTS * sub):

            @pl.when(has_down)
            def _():
                carry_copy(n).wait_recv()

            for hh in range(n * piece, (n + 1) * piece):
                h = p * quarter + hh
                state = carry[hh].astype(F32)
                for i in range(GROUP):
                    pr_send[i, hh] = state.astype(BF16)
                    d = jnp.exp(lastb[i, pl.ds(h, 1), :])
                    state = d * state + rs[i, hh].astype(F32)
                carry_out[hh] = state.astype(BF16)

            @pl.when(has_up)
            def _():
                carry_copy(n).start()

            if n % sub == sub - 1:
                for i in range(GROUP - 1):
                    prior_copy(n // sub, i).start()
        prior[p] = pr_send[p]

    def turn(r, _):
        zz = z - r

        @pl.when(r < z)
        def _():
            send_in_plane(zz - 1)

        next_column(r + 2)

        @pl.when(r == 0)
        def _():
            dk_copy(pd).wait_recv()
            dv_copy(pd).wait_recv()

        @pl.when(r > 0)
        def _():
            x_copy(zz, px).wait_recv()
            y_copy(zz, py).wait_recv()
            up_diagonal(zz).wait_recv()

        @pl.when(has_up)
        def _():
            up_diagonal(zz).start()

        @pl.when(r == z)
        def _():
            state_chain()

        @pl.when(r == 0)
        def _():
            attend(zz, True)

        @pl.when(r > 0)
        def _():
            attend(zz, False)

        return 0

    lax.fori_loop(0, z + 1, turn, 0)

    for g in range(kv_local):
        for t in range(tiles):
            cols = slice(t * MQ, (t + 1) * MQ)
            ot[g, cols, :] = (acc[g, :, cols] / l_ref[g, :, cols]).T

    rowsq[...] = jnp.zeros(rowsq.shape, F32)

    def outer(owner, j):
        hs = [j * part + u for u in range(part)]
        ids = [owner * quarter + hh for hh in hs]
        qh = [head_rows(qf, h).astype(BF16) for h in ids]
        old = [head_rows(mixed, h) for h in ids]
        ps = [prior[owner, hh] for hh in hs]
        os = [jnp.dot(q, x, preferred_element_type=F32) for q, x in zip(qh, ps)]
        new = [a + o * jnp.exp(colb[h]) for a, o, h in zip(old, os, ids)]
        for h, x in zip(ids, new):
            mixed[pl.ds(h, rows, stride=heads), :] = x
        rowsq[...] += sum(x * x for x in new)

    for j in range(PARTS):
        outer(p, j)
        for i in range(GROUP - 1):
            prior_copy(j, i).wait_recv()
            outer(peers[i], j)
    h_copies = [
        pltpu.make_async_remote_copy(
            src_ref=rowsq, dst_ref=rowsq_in.at[j - 1], send_sem=h_s.at[j - 1],
            recv_sem=h_r.at[j - 1], device_id={"head": (my_head + j) % heads_dev},
            device_id_type=MESH,
        )
        for j in range(1, heads_dev)
    ]
    for c in h_copies:
        c.start()

    def store_attn(i, _):
        t0 = pl.multiple_of(i * step, step)
        r0 = pl.multiple_of(t0 * group, step * group)
        parts = [
            ot[g, pl.ds(r0, step * group), :].reshape(step, group, HD) for g in range(kv_local)
        ]
        attn_out[pl.ds(t0, step)] = jnp.concatenate(parts, axis=1).astype(BF16)
        return 0

    lax.fori_loop(0, rows // step, store_attn, 0)
    attn_store = pltpu.make_async_copy(attn_out, attn_hbm, out_sem.at[0])
    attn_store.start()

    for c in h_copies:
        c.wait_recv()
    total = rowsq[...]
    for j in range(heads_dev - 1):
        total = total + rowsq_in[j]
    mean = jnp.sum(total, axis=1, keepdims=True) / (heads_dev * heads * HD)
    for c in h_copies:
        c.wait_send()
    rowsq[...] = jnp.broadcast_to(lax.rsqrt(mean + 1e-06), (rows, HD))

    def store_lin(i, _):
        t0 = pl.multiple_of(i * step, step)
        r0 = pl.multiple_of(t0 * heads, step * heads)
        x = mixed[pl.ds(r0, step * heads), :].reshape(step, heads, HD)
        inv = rowsq[pl.ds(t0, step), :].reshape(step, 1, HD)
        lin_out[pl.ds(t0, step)] = (x * inv * gain[...][None]).astype(BF16)
        return 0

    halves = 2
    lin_stores = []
    for j in range(halves):
        n = rows // step // halves
        lax.fori_loop(j * n, (j + 1) * n, store_lin, 0)
        own = pl.ds(j * n * step, n * step)
        lin_stores.append(
            pltpu.make_async_copy(lin_out.at[own], lin_hbm.at[own], out_sem.at[1 + j])
        )
        lin_stores[j].start()

    for c in last_copies + s1:
        c.wait_send()
    for j in range(PARTS):
        for i in range(GROUP - 1):
            prior_copy(j, i).wait_send()

    @pl.when(has_up)
    def _():
        for n in range(PARTS * sub):
            carry_copy(n).wait_send()

    def drain(zz, _):
        @pl.when(has_up)
        def _():
            up_copy(zz).wait_send()
            up_diagonal(zz).wait_send()

        x_copy(zz, p).wait_send()
        y_copy(zz, p).wait_send()
        return 0

    lax.fori_loop(0, z + 1, drain, 0)
    dk_copy(px).wait_send()
    dv_copy(py).wait_send()
    attn_store.wait()
    for c in lin_stores:
        c.wait()


def hand_over(lin_in, attn_in, lin_out, attn_out, sem):
    pieces = 4
    n = lin_in.shape[0] // pieces
    copies = []
    for i, (src, dst) in enumerate(((lin_in, lin_out), (attn_in, attn_out))):
        for j in range(pieces):
            own = pl.ds(j * n, n)
            copies.append(
                pltpu.make_async_copy(src.at[own], dst.at[own], sem.at[i * pieces + j])
            )
    for c in copies:
        c.start()
    for c in copies:
        c.wait()


def local(planes, heads_dev, lin_query, lin_key, lin_value, log_decay, norm_gain,
          attn_query, attn_key, attn_value):
    rows, heads, _ = lin_query.shape
    kv_local = attn_key.shape[1]
    group = heads // kv_local
    quarter = heads // GROUP
    vmem = pl.BlockSpec(memory_space=pltpu.VMEM)
    hbm = pl.BlockSpec(memory_space=pl.ANY)
    dma = pltpu.SemaphoreType.DMA
    out = jax.ShapeDtypeStruct(lin_query.shape, BF16)
    state = (GROUP, quarter, HD, HD)
    results = pl.pallas_call(
        functools.partial(kernel, planes, heads_dev),
        out_shape=(out, out),
        in_specs=[hbm, hbm, hbm, vmem, vmem, hbm, vmem, vmem],
        out_specs=(hbm, hbm),
        scratch_shapes=[pltpu.VMEM(lin_query.shape, BF16)] * 6
        + [dma((4,)), dma((3,))]
        + [pltpu.VMEM((rows * (-(-2 * kv_local // 8) * 8), HD), F32)]
        + [
            pltpu.VMEM((rows * heads, HD), F32),
            pltpu.VMEM((rows * heads, HD), F32),
            pltpu.VMEM((rows * heads, HD), F32),
            pltpu.VMEM((rows * heads, HD), F32),
            pltpu.VMEM((2, kv_local, planes, GROUP, rows, HD), BF16),
            pltpu.VMEM((kv_local, rows * group, HD), BF16),
            pltpu.VMEM((kv_local, HD, rows * group), F32),
            pltpu.VMEM((kv_local, 1, rows * group), F32),
            pltpu.VMEM((kv_local, 1, rows * group), F32),
            pltpu.VMEM((kv_local, rows * group, HD), F32),
            pltpu.VMEM((heads, rows), F32),
            pltpu.VMEM((heads, rows, rows), F32),
            pltpu.VMEM((GROUP, heads, HD), F32),
            pltpu.VMEM(state, BF16),
            pltpu.VMEM(state, BF16),
            pltpu.VMEM(state, BF16),
            pltpu.VMEM(state, BF16),
            pltpu.VMEM(state[1:], BF16),
            pltpu.VMEM(state[1:], BF16),
            pltpu.VMEM((rows, HD), F32),
            pltpu.VMEM((max(heads_dev - 1, 1), rows, HD), F32),
        ]
        + [dma((planes,))] * 8
        + [dma] * 4
        + [dma((GROUP - 1,))] * 4
        + [dma(((GROUP - 1) * PARTS,))] * 2
        + [dma((quarter,))] * 2
        + [dma((max(heads_dev - 1, 1),))] * 2,
        compiler_params=pltpu.CompilerParams(
            collective_id=0, has_side_effects=True, vmem_limit_bytes=56 * 2**20
        ),
        name="mixers",
    )(lin_query, lin_key, lin_value, log_decay, norm_gain, attn_query,
      attn_key, attn_value)
    return pl.pallas_call(
        hand_over,
        out_shape=(out, out),
        in_specs=[hbm, hbm],
        out_specs=(hbm, hbm),
        scratch_shapes=[dma((8,))],
        compiler_params=pltpu.CompilerParams(vmem_limit_bytes=56 * 2**20),
        name="hand_over",
    )(*results)


def solution(mesh):
    planes = mesh.shape["ctx"] // GROUP
    return jax.shard_map(
        functools.partial(local, planes, mesh.shape["head"]),
        mesh=mesh,
        in_specs=(
            P("ctx", "head", None),
            P("ctx", "head", None),
            P("ctx", "head", None),
            P("head", "ctx"),
            P("head", None),
            P("ctx", "head", None),
            P("ctx", "head", None),
            P("ctx", "head", None),
        ),
        out_specs=(P("ctx", "head", None), P("ctx", "head", None)),
        check_vma=False,
    )
```

```python
import functools
import math

import jax
import jax.numpy as jnp
from jax import lax
from jax.experimental import pallas as pl
from jax.experimental.pallas import tpu as pltpu
from jax.sharding import PartitionSpec as P

QUERY_HEADS = 64
HD = 128
GROUP = 4
F32 = jnp.float32
BF16 = jnp.bfloat16
MESH = pl.DeviceIdType.MESH
NT = (((1,), (1,)), ((), ()))
TN = (((0,), (0,)), ((), ()))
MQ = 256
PARTS = 2


def silu(x):
    half = 0.5 * x
    return half + half * jnp.tanh(half)


def kernel(
    planes, heads_dev, lq_in, lk_in, lv_in, decay, aq_in, k_in, v_in, mixed_hbm, inverse, attn_hbm,
    lq, lk, lv, aq, attn_out, in_sem, out_sem, by_row,
    qf, kf, vf, mixed, kv, qs, acc, m_ref, l_ref, ot, cum_ref, colb, lastb,
    sbuf, rs, prior, pr_send, carry, carry_out, rowsq, rowsq_in,
    z_s, z_r, zd_s, zd_r, x_s, x_r, y_s, y_r, dk_s, dk_r, dv_s, dv_r,
    s1_s, s1_r, la_s, la_r, s3_s, s3_r, c_s, c_r, h_s, h_r,
):
    loads = [
        pltpu.make_async_copy(src, dst, in_sem.at[i])
        for i, (src, dst) in enumerate(((lk_in, lk), (lv_in, lv), (aq_in, aq), (lq_in, lq)))
    ]
    for c in loads:
        c.start()
    rows, heads, _ = lq.shape
    kv_local = k_in.shape[1]
    group = heads // kv_local
    quarter = heads // GROUP
    me = lax.axis_index("ctx")
    my_head = lax.axis_index("head")
    z = me // GROUP
    p = me % GROUP
    base = z * GROUP
    px = jnp.where(p % 2 == 0, p + 1, p - 1)
    py = (p + 2) % GROUP
    pd = jnp.where(px >= 2, px - 2, px + 2)
    peers = (px, py, pd)
    has_up = z < planes - 1
    has_down = z > 0

    def remote(src, dst, s, r, ctx):
        return pltpu.make_async_remote_copy(
            src_ref=src, dst_ref=dst, send_sem=s, recv_sem=r,
            device_id={"ctx": ctx}, device_id_type=MESH,
        )

    slots = -(-2 * kv_local // 8) * 8
    both = [k_in[...].astype(F32), v_in[...].astype(F32)]
    if slots > 2 * kv_local:
        both.append(jnp.zeros((rows, slots - 2 * kv_local, HD), F32))
    by_row[...] = jnp.concatenate(both, axis=1).reshape(rows * slots, HD)
    for j in range(2):
        for g in range(kv_local):
            kv[j, g, z, p] = by_row[pl.ds(j * kv_local + g, rows, stride=slots), :].astype(BF16)

    barrier = pltpu.get_barrier_semaphore()
    for peer in peers:
        pl.semaphore_signal(barrier, inc=1, device_id={"ctx": base + peer}, device_id_type=MESH)
    for j in range(1, heads_dev):
        pl.semaphore_signal(
            barrier, inc=1, device_id={"head": (my_head + j) % heads_dev}, device_id_type=MESH
        )

    @pl.when(has_up)
    def _():
        pl.semaphore_signal(barrier, inc=1, device_id={"ctx": me + GROUP}, device_id_type=MESH)

    @pl.when(has_down)
    def _():
        pl.semaphore_signal(barrier, inc=1, device_id={"ctx": me - GROUP}, device_id_type=MESH)

    along = jnp.where(has_up, 1, 0) + jnp.where(has_down, 1, 0)
    pl.semaphore_wait(barrier, GROUP - 1 + heads_dev - 1 + along)

    def block(zz, col):
        return kv.at[:, :, zz, col]

    def up_copy(zz):
        return remote(block(zz, p), block(zz, p), z_s.at[zz], z_r.at[zz], me + GROUP)

    def up_diagonal(zz):
        return remote(block(zz, pd), block(zz, pd), zd_s.at[zz], zd_r.at[zz], me + GROUP)

    def x_copy(zz, col):
        return remote(block(zz, col), block(zz, col), x_s.at[zz], x_r.at[zz], base + px)

    def y_copy(zz, col):
        return remote(block(zz, col), block(zz, col), y_s.at[zz], y_r.at[zz], base + py)

    def dk_copy(col):
        return remote(kv.at[0, :, z, col], kv.at[0, :, z, col], dk_s, dk_r, base + py)

    def dv_copy(col):
        return remote(kv.at[1, :, z, col], kv.at[1, :, z, col], dv_s, dv_r, base + px)

    def send_in_plane(zz):
        x_copy(zz, p).start()
        y_copy(zz, p).start()

    def send_up(zz):
        @pl.when(has_up)
        def _():
            up_copy(zz).start()

    send_in_plane(z)
    send_up(z)

    step = 16

    def activate(src, dst):
        def body(i, _):
            t0 = pl.multiple_of(i * step, step)
            x = silu(src[pl.ds(t0, step)].astype(F32))
            r0 = pl.multiple_of(t0 * heads, step * heads)
            dst[pl.ds(r0, step * heads), :] = x.reshape(step * heads, HD)
            return 0

        lax.fori_loop(0, rows // step, body, 0)

    def head_rows(ref, h):
        return ref[pl.ds(h, rows, stride=heads), :]

    row_id = lax.broadcasted_iota(jnp.int32, (rows, rows), 0)
    col_id = lax.broadcasted_iota(jnp.int32, (rows, rows), 1)
    upper = jnp.where(row_id <= col_id, 1.0, 0.0).astype(F32)
    cum_all = lax.dot_general(
        decay[...], upper, (((1,), (0,)), ((), ())),
        precision=lax.Precision.HIGHEST, preferred_element_type=F32,
    )
    cum_ref[...] = cum_all
    lastb[p] = jnp.broadcast_to(cum_all[:, rows - 1 : rows], (heads, HD))
    last_copies = [
        remote(lastb.at[p], lastb.at[p], la_s.at[i], la_r.at[i], base + peer)
        for i, peer in enumerate(peers)
    ]
    for c in last_copies:
        c.start()

    loads[0].wait()
    activate(lk, kf)
    loads[1].wait()
    activate(lv, vf)

    together = min(4, quarter)

    def cum_row(h):
        return jnp.broadcast_to(cum_ref[pl.ds(h, 1), :], (rows, rows))

    def local_states(owner):
        def body(i, _):
            hs = [i * together + u for u in range(together)]
            ids = [owner * quarter + hh for hh in hs]
            ks = [head_rows(kf, h).astype(BF16).astype(F32) for h in ids]
            vs = [head_rows(vf, h).astype(BF16) for h in ids]
            lasts = [jnp.broadcast_to(lastb[p, pl.ds(h, 1), :], (rows, HD)) for h in ids]
            cols = [cum_row(h).T for h in ids]
            sks = [(k * jnp.exp(a - c)).astype(BF16) for k, a, c in zip(ks, lasts, cols)]
            sts = [
                lax.dot_general(sk, v, TN, preferred_element_type=F32) for sk, v in zip(sks, vs)
            ]
            for h, c in zip(ids, cols):
                colb[h] = c
            for hh, st in zip(hs, sts):
                sbuf[owner, hh] = st.astype(BF16)
            return 0

        lax.fori_loop(0, quarter // together, body, 0)

    s1 = [
        remote(sbuf.at[peer], rs.at[p], s1_s.at[i], s1_r.at[i], base + peer)
        for i, peer in enumerate(peers)
    ]
    for peer, c in zip(peers, s1):
        local_states(peer)
        c.start()
    local_states(p)

    def next_column(r):
        @pl.when(r <= z)
        def _():
            up_copy(z - r).wait_recv()
            send_up(z - r)

    x_copy(z, px).wait_recv()
    dk_copy(px).start()
    y_copy(z, py).wait_recv()
    dv_copy(py).start()
    next_column(1)

    def load_queries(i, _):
        t0 = pl.multiple_of(i * step, step)
        x = aq[pl.ds(t0, step)].astype(F32)
        for g in range(kv_local):
            part = x[:, g * group : (g + 1) * group, :].reshape(step * group, HD)
            r0 = pl.multiple_of(t0 * group, step * group)
            qs[g, pl.ds(r0, step * group), :] = part.astype(BF16)
        return 0

    loads[2].wait()
    lax.fori_loop(0, rows // step, load_queries, 0)
    loads[3].wait()
    activate(lq, qf)

    dk_copy(pd).wait_recv()
    dv_copy(pd).wait_recv()

    @pl.when(has_up)
    def _():
        up_diagonal(z).start()

    def inner(i, _):
        ids = [i * together + u for u in range(together)]
        qh = [head_rows(qf, h).astype(BF16) for h in ids]
        ks = [head_rows(kf, h).astype(BF16) for h in ids]
        vs = [head_rows(vf, h).astype(BF16) for h in ids]
        spread = [colb[h] - cum_row(h) for h in ids]
        sc = [lax.dot_general(q, k, NT, preferred_element_type=F32) for q, k in zip(qh, ks)]
        dm = [jnp.exp(jnp.where(row_id >= col_id, d, -1e30)) for d in spread]
        ws = [(a * d).astype(BF16) for a, d in zip(sc, dm)]
        outs = [jnp.dot(w, v, preferred_element_type=F32) for w, v in zip(ws, vs)]
        for h, o in zip(ids, outs):
            mixed[pl.ds(h, rows, stride=heads), :] = o
        return 0

    lax.fori_loop(0, heads // together, inner, 0)

    m_ref[...] = jnp.full(m_ref.shape, -1e30, F32)
    l_ref[...] = jnp.zeros(l_ref.shape, F32)
    acc[...] = jnp.zeros(acc.shape, F32)
    scale = HD ** (-0.5) * math.log2(math.e)
    span = GROUP * rows
    tiles = rows * group // MQ

    def attend(zz, masked):
        def body(g, _):
            cols = [pl.ds(t * MQ, MQ) for t in range(tiles)]
            k = kv[0, g, zz].reshape(span, HD)
            v = kv[1, g, zz].reshape(span, HD)
            m_old = [m_ref[g, :, c] for c in cols]
            l_old = [l_ref[g, :, c] for c in cols]

            def scores(t):
                s = lax.dot_general(k, qs[g, cols[t], :], NT, preferred_element_type=F32) * scale
                if masked:
                    key_pos = lax.broadcasted_iota(jnp.int32, (span, MQ), 0)
                    col_pos = lax.broadcasted_iota(jnp.int32, (1, MQ), 1)
                    s = jnp.where(key_pos <= p * rows + (t * MQ + col_pos) // group, s, -1e30)
                return s

            def probs(t, s):
                m_new = jnp.maximum(m_old[t], jnp.max(s, axis=0, keepdims=True))
                alpha = jnp.exp2(m_old[t] - m_new)
                e = jnp.exp2(s - m_new)
                m_ref[g, :, cols[t]] = m_new
                l_ref[g, :, cols[t]] = l_old[t] * alpha + jnp.sum(e, axis=0, keepdims=True)
                return e.astype(BF16), alpha

            def values(t, e, alpha):
                o = lax.dot_general(v, e, TN, preferred_element_type=F32)
                acc[g, :, cols[t]] = acc[g, :, cols[t]] * alpha + o

            ss, es = {}, {}
            for t in range(tiles + 2):
                if t < tiles:
                    ss[t] = scores(t)
                if 0 <= t - 2 < tiles:
                    values(t - 2, *es.pop(t - 2))
                if 0 <= t - 1 < tiles:
                    es[t - 1] = probs(t - 1, ss.pop(t - 1))
            return 0

        lax.fori_loop(0, kv_local, body, 0)

    part = quarter // PARTS

    sub = 2 if part % 2 == 0 else 1
    piece = part // sub

    def carry_copy(n):
        own = pl.ds(n * piece, piece)
        return remote(carry_out.at[own], carry.at[own], c_s.at[n], c_r.at[n], me + GROUP)

    def prior_copy(j, i):
        own = pl.ds(j * part, part)
        n = j * (GROUP - 1) + i
        return remote(
            pr_send.at[peers[i], own], prior.at[p, own], s3_s.at[n], s3_r.at[n], base + peers[i]
        )

    def state_chain():
        for i in range(GROUP - 1):
            s1[i].wait_recv()
            last_copies[i].wait_recv()
        rs[p] = sbuf[p]

        @pl.when(jnp.logical_not(has_down))
        def _():
            carry[...] = jnp.zeros(carry.shape, BF16)

        for n in range(PARTS * sub):

            @pl.when(has_down)
            def _():
                carry_copy(n).wait_recv()

            for hh in range(n * piece, (n + 1) * piece):
                h = p * quarter + hh
                state = carry[hh].astype(F32)
                for i in range(GROUP):
                    pr_send[i, hh] = state.astype(BF16)
                    d = jnp.exp(lastb[i, pl.ds(h, 1), :])
                    state = d * state + rs[i, hh].astype(F32)
                carry_out[hh] = state.astype(BF16)

            @pl.when(has_up)
            def _():
                carry_copy(n).start()

            if n % sub == sub - 1:
                for i in range(GROUP - 1):
                    prior_copy(n // sub, i).start()
        prior[p] = pr_send[p]

    def turn(r, _):
        zz = z - r

        @pl.when(r < z)
        def _():
            send_in_plane(zz - 1)

        next_column(r + 2)

        @pl.when(r > 0)
        def _():
            up_diagonal(zz).wait_recv()

            @pl.when(has_up)
            def _():
                up_diagonal(zz).start()

            x_copy(zz, px).wait_recv()
            y_copy(zz, py).wait_recv()

        @pl.when(r == z)
        def _():
            state_chain()

        @pl.when(r == 0)
        def _():
            attend(zz, True)

        @pl.when(r > 0)
        def _():
            attend(zz, False)

        return 0

    lax.fori_loop(0, z + 1, turn, 0)

    for g in range(kv_local):
        for t in range(tiles):
            cols = slice(t * MQ, (t + 1) * MQ)
            ot[g, cols, :] = (acc[g, :, cols] / l_ref[g, :, cols]).T

    rowsq[...] = jnp.zeros(rowsq.shape, F32)

    def outer(owner, j):
        hs = [j * part + u for u in range(part)]
        ids = [owner * quarter + hh for hh in hs]
        qh = [head_rows(qf, h).astype(BF16) for h in ids]
        old = [head_rows(mixed, h) for h in ids]
        ps = [prior[owner, hh] for hh in hs]
        os = [jnp.dot(q, x, preferred_element_type=F32) for q, x in zip(qh, ps)]
        new = [a + o * jnp.exp(colb[h]) for a, o, h in zip(old, os, ids)]
        for h, x in zip(ids, new):
            mixed[pl.ds(h, rows, stride=heads), :] = x
        rowsq[...] += sum(x * x for x in new)

    for j in range(PARTS):
        outer(p, j)
        for i in range(GROUP - 1):
            prior_copy(j, i).wait_recv()
            outer(peers[i], j)
    h_copies = [
        pltpu.make_async_remote_copy(
            src_ref=rowsq, dst_ref=rowsq_in.at[j - 1], send_sem=h_s.at[j - 1],
            recv_sem=h_r.at[j - 1], device_id={"head": (my_head + j) % heads_dev},
            device_id_type=MESH,
        )
        for j in range(1, heads_dev)
    ]
    for c in h_copies:
        c.start()
    mixed_store = pltpu.make_async_copy(mixed, mixed_hbm, out_sem.at[1])
    mixed_store.start()

    def store_attn(i, _):
        t0 = pl.multiple_of(i * step, step)
        r0 = pl.multiple_of(t0 * group, step * group)
        parts = [
            ot[g, pl.ds(r0, step * group), :].reshape(step, group, HD) for g in range(kv_local)
        ]
        attn_out[pl.ds(t0, step)] = jnp.concatenate(parts, axis=1).astype(BF16)
        return 0

    lax.fori_loop(0, rows // step, store_attn, 0)
    attn_store = pltpu.make_async_copy(attn_out, attn_hbm, out_sem.at[0])
    attn_store.start()

    for c in h_copies:
        c.wait_recv()
    total = rowsq[...]
    for j in range(heads_dev - 1):
        total = total + rowsq_in[j]
    mean = jnp.sum(total, axis=1, keepdims=True) / (heads_dev * heads * HD)
    inverse[...] = jnp.broadcast_to(lax.rsqrt(mean + 1e-06), (rows, HD))

    for c in last_copies + s1:
        c.wait_send()
    for j in range(PARTS):
        for i in range(GROUP - 1):
            prior_copy(j, i).wait_send()

    @pl.when(has_up)
    def _():
        for n in range(PARTS * sub):
            carry_copy(n).wait_send()

    def drain(zz, _):
        @pl.when(has_up)
        def _():
            up_copy(zz).wait_send()
            up_diagonal(zz).wait_send()

        x_copy(zz, p).wait_send()
        y_copy(zz, p).wait_send()
        return 0

    lax.fori_loop(0, z + 1, drain, 0)
    dk_copy(px).wait_send()
    dv_copy(py).wait_send()
    for c in h_copies:
        c.wait_send()
    attn_store.wait()
    mixed_store.wait()


def finish(mixed, inverse, gain, attn_in, lin_out, attn_out):
    inv = inverse[...].reshape(inverse.shape[0], 1, HD)
    lin_out[...] = (mixed[...] * inv * gain[...][None]).astype(BF16)
    attn_out[...] = attn_in[...]


def local(planes, heads_dev, lin_query, lin_key, lin_value, log_decay, norm_gain,
          attn_query, attn_key, attn_value):
    rows, heads, _ = lin_query.shape
    kv_local = attn_key.shape[1]
    group = heads // kv_local
    quarter = heads // GROUP
    vmem = pl.BlockSpec(memory_space=pltpu.VMEM)
    hbm = pl.BlockSpec(memory_space=pl.ANY)
    dma = pltpu.SemaphoreType.DMA
    out = jax.ShapeDtypeStruct(lin_query.shape, BF16)
    state = (GROUP, quarter, HD, HD)
    mixed, inverse, attn = pl.pallas_call(
        functools.partial(kernel, planes, heads_dev),
        out_shape=(
            jax.ShapeDtypeStruct((rows * heads, HD), F32),
            jax.ShapeDtypeStruct((rows, HD), F32),
            out,
        ),
        in_specs=[hbm, hbm, hbm, vmem, hbm, vmem, vmem],
        out_specs=(hbm, vmem, hbm),
        scratch_shapes=[pltpu.VMEM(lin_query.shape, BF16)] * 5
        + [dma((4,)), dma((2,))]
        + [pltpu.VMEM((rows * (-(-2 * kv_local // 8) * 8), HD), F32)]
        + [
            pltpu.VMEM((rows * heads, HD), F32),
            pltpu.VMEM((rows * heads, HD), F32),
            pltpu.VMEM((rows * heads, HD), F32),
            pltpu.VMEM((rows * heads, HD), F32),
            pltpu.VMEM((2, kv_local, planes, GROUP, rows, HD), BF16),
            pltpu.VMEM((kv_local, rows * group, HD), BF16),
            pltpu.VMEM((kv_local, HD, rows * group), F32),
            pltpu.VMEM((kv_local, 1, rows * group), F32),
            pltpu.VMEM((kv_local, 1, rows * group), F32),
            pltpu.VMEM((kv_local, rows * group, HD), F32),
            pltpu.VMEM((heads, rows), F32),
            pltpu.VMEM((heads, rows, rows), F32),
            pltpu.VMEM((GROUP, heads, HD), F32),
            pltpu.VMEM(state, BF16),
            pltpu.VMEM(state, BF16),
            pltpu.VMEM(state, BF16),
            pltpu.VMEM(state, BF16),
            pltpu.VMEM(state[1:], BF16),
            pltpu.VMEM(state[1:], BF16),
            pltpu.VMEM((rows, HD), F32),
            pltpu.VMEM((max(heads_dev - 1, 1), rows, HD), F32),
        ]
        + [dma((planes,))] * 8
        + [dma] * 4
        + [dma((GROUP - 1,))] * 4
        + [dma(((GROUP - 1) * PARTS,))] * 2
        + [dma((quarter,))] * 2
        + [dma((max(heads_dev - 1, 1),))] * 2,
        compiler_params=pltpu.CompilerParams(
            collective_id=0, has_side_effects=True, vmem_limit_bytes=56 * 2**20
        ),
        name="mixers",
    )(lin_query, lin_key, lin_value, log_decay, attn_query,
      attn_key, attn_value)
    tile = rows // 4
    block = pl.BlockSpec((tile, heads, HD), lambda i: (i, 0, 0))
    return pl.pallas_call(
        finish,
        grid=(rows // tile,),
        out_shape=(out, out),
        in_specs=[
            block,
            pl.BlockSpec((tile, HD), lambda i: (i, 0)),
            pl.BlockSpec((heads, HD), lambda i: (0, 0)),
            block,
        ],
        out_specs=(block, block),
        compiler_params=pltpu.CompilerParams(vmem_limit_bytes=56 * 2**20),
        name="finish",
    )(mixed.reshape(rows, heads, HD), inverse, norm_gain, attn)


def solution(mesh):
    planes = mesh.shape["ctx"] // GROUP
    return jax.shard_map(
        functools.partial(local, planes, mesh.shape["head"]),
        mesh=mesh,
        in_specs=(
            P("ctx", "head", None),
            P("ctx", "head", None),
            P("ctx", "head", None),
            P("head", "ctx"),
            P("head", None),
            P("ctx", "head", None),
            P("ctx", "head", None),
            P("ctx", "head", None),
        ),
        out_specs=(P("ctx", "head", None), P("ctx", "head", None)),
        check_vma=False,
    )
```

```python
import functools
import math

import jax
import jax.numpy as jnp
from jax import lax
from jax.experimental import pallas as pl
from jax.experimental.pallas import tpu as pltpu
from jax.sharding import PartitionSpec as P

QUERY_HEADS = 64
HD = 128
GROUP = 4
F32 = jnp.float32
BF16 = jnp.bfloat16
MESH = pl.DeviceIdType.MESH
NT = (((1,), (1,)), ((), ()))
TN = (((0,), (0,)), ((), ()))
MQ = 256
PARTS = 2


def silu(x):
    half = 0.5 * x
    return half + half * jnp.tanh(half)


def kernel(
    planes, heads_dev, lq_in, lk_in, lv_in, decay, gain, aq_in, k_in, v_in, lin_hbm, attn_hbm,
    lq, lk, lv, aq, lin_out, attn_out, in_sem, out_sem, by_row,
    qf, kf, vf, mixed, kv, qs, acc, m_ref, l_ref, ot, cum_ref, colb, lastb,
    sbuf, rs, prior, pr_send, carry, carry_out, rowsq, rowsq_in,
    z_s, z_r, zd_s, zd_r, x_s, x_r, y_s, y_r, dk_s, dk_r, dv_s, dv_r,
    s1_s, s1_r, la_s, la_r, s3_s, s3_r, c_s, c_r, h_s, h_r,
):
    loads = [
        pltpu.make_async_copy(src, dst, in_sem.at[i])
        for i, (src, dst) in enumerate(((lk_in, lk), (lv_in, lv), (aq_in, aq), (lq_in, lq)))
    ]
    for c in loads:
        c.start()
    rows, heads, _ = lq.shape
    kv_local = k_in.shape[1]
    group = heads // kv_local
    quarter = heads // GROUP
    me = lax.axis_index("ctx")
    my_head = lax.axis_index("head")
    z = me // GROUP
    p = me % GROUP
    base = z * GROUP
    px = jnp.where(p % 2 == 0, p + 1, p - 1)
    py = (p + 2) % GROUP
    pd = jnp.where(px >= 2, px - 2, px + 2)
    peers = (px, py, pd)
    has_up = z < planes - 1
    has_down = z > 0

    def remote(src, dst, s, r, ctx):
        return pltpu.make_async_remote_copy(
            src_ref=src, dst_ref=dst, send_sem=s, recv_sem=r,
            device_id={"ctx": ctx}, device_id_type=MESH,
        )

    slots = -(-2 * kv_local // 8) * 8
    both = [k_in[...].astype(F32), v_in[...].astype(F32)]
    if slots > 2 * kv_local:
        both.append(jnp.zeros((rows, slots - 2 * kv_local, HD), F32))
    by_row[...] = jnp.concatenate(both, axis=1).reshape(rows * slots, HD)
    for j in range(2):
        for g in range(kv_local):
            kv[j, g, z, p] = by_row[pl.ds(j * kv_local + g, rows, stride=slots), :].astype(BF16)

    barrier = pltpu.get_barrier_semaphore()
    for peer in peers:
        pl.semaphore_signal(barrier, inc=1, device_id={"ctx": base + peer}, device_id_type=MESH)
    for j in range(1, heads_dev):
        pl.semaphore_signal(
            barrier, inc=1, device_id={"head": (my_head + j) % heads_dev}, device_id_type=MESH
        )

    @pl.when(has_up)
    def _():
        pl.semaphore_signal(barrier, inc=1, device_id={"ctx": me + GROUP}, device_id_type=MESH)

    @pl.when(has_down)
    def _():
        pl.semaphore_signal(barrier, inc=1, device_id={"ctx": me - GROUP}, device_id_type=MESH)

    along = jnp.where(has_up, 1, 0) + jnp.where(has_down, 1, 0)
    pl.semaphore_wait(barrier, GROUP - 1 + heads_dev - 1 + along)

    def block(zz, col):
        return kv.at[:, :, zz, col]

    def up_copy(zz):
        return remote(block(zz, p), block(zz, p), z_s.at[zz], z_r.at[zz], me + GROUP)

    def up_diagonal(zz):
        return remote(block(zz, pd), block(zz, pd), zd_s.at[zz], zd_r.at[zz], me + GROUP)

    def x_copy(zz, col):
        return remote(block(zz, col), block(zz, col), x_s.at[zz], x_r.at[zz], base + px)

    def y_copy(zz, col):
        return remote(block(zz, col), block(zz, col), y_s.at[zz], y_r.at[zz], base + py)

    def dk_copy(col):
        return remote(kv.at[0, :, z, col], kv.at[0, :, z, col], dk_s, dk_r, base + py)

    def dv_copy(col):
        return remote(kv.at[1, :, z, col], kv.at[1, :, z, col], dv_s, dv_r, base + px)

    def send_in_plane(zz):
        x_copy(zz, p).start()
        y_copy(zz, p).start()

    def send_up(zz):
        @pl.when(has_up)
        def _():
            up_copy(zz).start()

    send_in_plane(z)
    send_up(z)

    step = 16

    def activate(src, dst):
        def body(i, _):
            t0 = pl.multiple_of(i * step, step)
            x = silu(src[pl.ds(t0, step)].astype(F32))
            r0 = pl.multiple_of(t0 * heads, step * heads)
            dst[pl.ds(r0, step * heads), :] = x.reshape(step * heads, HD)
            return 0

        lax.fori_loop(0, rows // step, body, 0)

    def head_rows(ref, h):
        return ref[pl.ds(h, rows, stride=heads), :]

    row_id = lax.broadcasted_iota(jnp.int32, (rows, rows), 0)
    col_id = lax.broadcasted_iota(jnp.int32, (rows, rows), 1)
    upper = jnp.where(row_id <= col_id, 1.0, 0.0).astype(F32)
    cum_all = lax.dot_general(
        decay[...], upper, (((1,), (0,)), ((), ())),
        precision=lax.Precision.HIGHEST, preferred_element_type=F32,
    )
    cum_ref[...] = cum_all
    lastb[p] = jnp.broadcast_to(cum_all[:, rows - 1 : rows], (heads, HD))
    last_copies = [
        remote(lastb.at[p], lastb.at[p], la_s.at[i], la_r.at[i], base + peer)
        for i, peer in enumerate(peers)
    ]
    for c in last_copies:
        c.start()

    loads[0].wait()
    activate(lk, kf)
    loads[1].wait()
    activate(lv, vf)

    together = min(4, quarter)

    def cum_row(h):
        return jnp.broadcast_to(cum_ref[pl.ds(h, 1), :], (rows, rows))

    def local_states(owner):
        def body(i, _):
            hs = [i * together + u for u in range(together)]
            ids = [owner * quarter + hh for hh in hs]
            ks = [head_rows(kf, h).astype(BF16).astype(F32) for h in ids]
            vs = [head_rows(vf, h).astype(BF16) for h in ids]
            lasts = [jnp.broadcast_to(lastb[p, pl.ds(h, 1), :], (rows, HD)) for h in ids]
            cols = [cum_row(h).T for h in ids]
            sks = [(k * jnp.exp(a - c)).astype(BF16) for k, a, c in zip(ks, lasts, cols)]
            sts = [
                lax.dot_general(sk, v, TN, preferred_element_type=F32) for sk, v in zip(sks, vs)
            ]
            for h, c in zip(ids, cols):
                colb[h] = c
            for hh, st in zip(hs, sts):
                sbuf[owner, hh] = st.astype(BF16)
            return 0

        lax.fori_loop(0, quarter // together, body, 0)

    s1 = [
        remote(sbuf.at[peer], rs.at[p], s1_s.at[i], s1_r.at[i], base + peer)
        for i, peer in enumerate(peers)
    ]
    for peer, c in zip(peers, s1):
        local_states(peer)
        c.start()
    local_states(p)

    def next_column(r):
        @pl.when(r <= z)
        def _():
            up_copy(z - r).wait_recv()
            send_up(z - r)

    x_copy(z, px).wait_recv()
    dk_copy(px).start()
    y_copy(z, py).wait_recv()
    dv_copy(py).start()
    next_column(1)

    def load_queries(i, _):
        t0 = pl.multiple_of(i * step, step)
        x = aq[pl.ds(t0, step)].astype(F32)
        for g in range(kv_local):
            part = x[:, g * group : (g + 1) * group, :].reshape(step * group, HD)
            r0 = pl.multiple_of(t0 * group, step * group)
            qs[g, pl.ds(r0, step * group), :] = part.astype(BF16)
        return 0

    loads[2].wait()
    lax.fori_loop(0, rows // step, load_queries, 0)
    loads[3].wait()
    activate(lq, qf)

    def inner(i, _):
        ids = [i * together + u for u in range(together)]
        qh = [head_rows(qf, h).astype(BF16) for h in ids]
        ks = [head_rows(kf, h).astype(BF16) for h in ids]
        vs = [head_rows(vf, h).astype(BF16) for h in ids]
        spread = [colb[h] - cum_row(h) for h in ids]
        sc = [lax.dot_general(q, k, NT, preferred_element_type=F32) for q, k in zip(qh, ks)]
        dm = [jnp.exp(jnp.where(row_id >= col_id, d, -1e30)) for d in spread]
        ws = [(a * d).astype(BF16) for a, d in zip(sc, dm)]
        outs = [jnp.dot(w, v, preferred_element_type=F32) for w, v in zip(ws, vs)]
        for h, o in zip(ids, outs):
            mixed[pl.ds(h, rows, stride=heads), :] = o
        return 0

    lax.fori_loop(0, heads // together, inner, 0)

    m_ref[...] = jnp.full(m_ref.shape, -1e30, F32)
    l_ref[...] = jnp.zeros(l_ref.shape, F32)
    acc[...] = jnp.zeros(acc.shape, F32)
    scale = HD ** (-0.5) * math.log2(math.e)
    span = GROUP * rows
    tiles = rows * group // MQ

    def attend(zz, masked):
        def body(g, _):
            cols = [pl.ds(t * MQ, MQ) for t in range(tiles)]
            k = kv[0, g, zz].reshape(span, HD)
            v = kv[1, g, zz].reshape(span, HD)
            m_old = [m_ref[g, :, c] for c in cols]
            l_old = [l_ref[g, :, c] for c in cols]

            def scores(t):
                s = lax.dot_general(k, qs[g, cols[t], :], NT, preferred_element_type=F32) * scale
                if masked:
                    key_pos = lax.broadcasted_iota(jnp.int32, (span, MQ), 0)
                    col_pos = lax.broadcasted_iota(jnp.int32, (1, MQ), 1)
                    s = jnp.where(key_pos <= p * rows + (t * MQ + col_pos) // group, s, -1e30)
                return s

            def probs(t, s):
                m_new = jnp.maximum(m_old[t], jnp.max(s, axis=0, keepdims=True))
                alpha = jnp.exp2(m_old[t] - m_new)
                e = jnp.exp2(s - m_new)
                m_ref[g, :, cols[t]] = m_new
                l_ref[g, :, cols[t]] = l_old[t] * alpha + jnp.sum(e, axis=0, keepdims=True)
                return e.astype(BF16), alpha

            def values(t, e, alpha):
                o = lax.dot_general(v, e, TN, preferred_element_type=F32)
                acc[g, :, cols[t]] = acc[g, :, cols[t]] * alpha + o

            ss, es = {}, {}
            for t in range(tiles + 2):
                if t < tiles:
                    ss[t] = scores(t)
                if 0 <= t - 2 < tiles:
                    values(t - 2, *es.pop(t - 2))
                if 0 <= t - 1 < tiles:
                    es[t - 1] = probs(t - 1, ss.pop(t - 1))
            return 0

        lax.fori_loop(0, kv_local, body, 0)

    part = quarter // PARTS

    sub = 2 if part % 2 == 0 else 1
    piece = part // sub

    def carry_copy(n):
        own = pl.ds(n * piece, piece)
        return remote(carry_out.at[own], carry.at[own], c_s.at[n], c_r.at[n], me + GROUP)

    def prior_copy(j, i):
        own = pl.ds(j * part, part)
        n = j * (GROUP - 1) + i
        return remote(
            pr_send.at[peers[i], own], prior.at[p, own], s3_s.at[n], s3_r.at[n], base + peers[i]
        )

    def state_chain():
        for i in range(GROUP - 1):
            s1[i].wait_recv()
            last_copies[i].wait_recv()
        rs[p] = sbuf[p]

        @pl.when(jnp.logical_not(has_down))
        def _():
            carry[...] = jnp.zeros(carry.shape, BF16)

        for n in range(PARTS * sub):

            @pl.when(has_down)
            def _():
                carry_copy(n).wait_recv()

            for hh in range(n * piece, (n + 1) * piece):
                h = p * quarter + hh
                state = carry[hh].astype(F32)
                for i in range(GROUP):
                    pr_send[i, hh] = state.astype(BF16)
                    d = jnp.exp(lastb[i, pl.ds(h, 1), :])
                    state = d * state + rs[i, hh].astype(F32)
                carry_out[hh] = state.astype(BF16)

            @pl.when(has_up)
            def _():
                carry_copy(n).start()

            if n % sub == sub - 1:
                for i in range(GROUP - 1):
                    prior_copy(n // sub, i).start()
        prior[p] = pr_send[p]

    def turn(r, _):
        zz = z - r

        @pl.when(r < z)
        def _():
            send_in_plane(zz - 1)

        next_column(r + 2)

        @pl.when(r == 0)
        def _():
            dk_copy(pd).wait_recv()
            dv_copy(pd).wait_recv()

        @pl.when(r > 0)
        def _():
            x_copy(zz, px).wait_recv()
            y_copy(zz, py).wait_recv()
            up_diagonal(zz).wait_recv()

        @pl.when(has_up)
        def _():
            up_diagonal(zz).start()

        @pl.when(r == z)
        def _():
            state_chain()

        @pl.when(r == 0)
        def _():
            attend(zz, True)

        @pl.when(r > 0)
        def _():
            attend(zz, False)

        return 0

    lax.fori_loop(0, z + 1, turn, 0)

    for g in range(kv_local):
        for t in range(tiles):
            cols = slice(t * MQ, (t + 1) * MQ)
            ot[g, cols, :] = (acc[g, :, cols] / l_ref[g, :, cols]).T

    rowsq[...] = jnp.zeros(rowsq.shape, F32)

    def outer(owner, j):
        hs = [j * part + u for u in range(part)]
        ids = [owner * quarter + hh for hh in hs]
        qh = [head_rows(qf, h).astype(BF16) for h in ids]
        old = [head_rows(mixed, h) for h in ids]
        ps = [prior[owner, hh] for hh in hs]
        os = [jnp.dot(q, x, preferred_element_type=F32) for q, x in zip(qh, ps)]
        new = [a + o * jnp.exp(colb[h]) for a, o, h in zip(old, os, ids)]
        for h, x in zip(ids, new):
            mixed[pl.ds(h, rows, stride=heads), :] = x
        rowsq[...] += sum(x * x for x in new)

    for j in range(PARTS):
        outer(p, j)
        for i in range(GROUP - 1):
            prior_copy(j, i).wait_recv()
            outer(peers[i], j)
    h_copies = [
        pltpu.make_async_remote_copy(
            src_ref=rowsq, dst_ref=rowsq_in.at[j - 1], send_sem=h_s.at[j - 1],
            recv_sem=h_r.at[j - 1], device_id={"head": (my_head + j) % heads_dev},
            device_id_type=MESH,
        )
        for j in range(1, heads_dev)
    ]
    for c in h_copies:
        c.start()

    def store_attn(i, _):
        t0 = pl.multiple_of(i * step, step)
        r0 = pl.multiple_of(t0 * group, step * group)
        parts = [
            ot[g, pl.ds(r0, step * group), :].reshape(step, group, HD) for g in range(kv_local)
        ]
        attn_out[pl.ds(t0, step)] = jnp.concatenate(parts, axis=1).astype(BF16)
        return 0

    lax.fori_loop(0, rows // step, store_attn, 0)
    attn_store = pltpu.make_async_copy(attn_out, attn_hbm, out_sem.at[0])
    attn_store.start()

    for c in h_copies:
        c.wait_recv()
    total = rowsq[...]
    for j in range(heads_dev - 1):
        total = total + rowsq_in[j]
    mean = jnp.sum(total, axis=1, keepdims=True) / (heads_dev * heads * HD)
    for c in h_copies:
        c.wait_send()
    rowsq[...] = jnp.broadcast_to(lax.rsqrt(mean + 1e-06), (rows, HD))

    def store_lin(i, _):
        t0 = pl.multiple_of(i * step, step)
        r0 = pl.multiple_of(t0 * heads, step * heads)
        x = mixed[pl.ds(r0, step * heads), :].reshape(step, heads, HD)
        inv = rowsq[pl.ds(t0, step), :].reshape(step, 1, HD)
        lin_out[pl.ds(t0, step)] = (x * inv * gain[...][None]).astype(BF16)
        return 0

    halves = 2
    lin_stores = []
    for j in range(halves):
        n = rows // step // halves
        lax.fori_loop(j * n, (j + 1) * n, store_lin, 0)
        own = pl.ds(j * n * step, n * step)
        lin_stores.append(
            pltpu.make_async_copy(lin_out.at[own], lin_hbm.at[own], out_sem.at[1 + j])
        )
        lin_stores[j].start()

    for c in last_copies + s1:
        c.wait_send()
    for j in range(PARTS):
        for i in range(GROUP - 1):
            prior_copy(j, i).wait_send()

    @pl.when(has_up)
    def _():
        for n in range(PARTS * sub):
            carry_copy(n).wait_send()

    def drain(zz, _):
        @pl.when(has_up)
        def _():
            up_copy(zz).wait_send()
            up_diagonal(zz).wait_send()

        x_copy(zz, p).wait_send()
        y_copy(zz, p).wait_send()
        return 0

    lax.fori_loop(0, z + 1, drain, 0)
    dk_copy(px).wait_send()
    dv_copy(py).wait_send()
    attn_store.wait()
    for c in lin_stores:
        c.wait()


def hand_over(lin_in, attn_in, lin_out, attn_out, lin_held, attn_held, load_sem, store_sem):
    pieces = 4
    n = lin_in.shape[0] // pieces
    loads, stores = [], []
    arrays = ((lin_in, lin_held, lin_out), (attn_in, attn_held, attn_out))
    for i, (src, held, dst) in enumerate(arrays):
        for j in range(pieces):
            own, k = pl.ds(j * n, n), i * pieces + j
            loads.append(pltpu.make_async_copy(src.at[own], held.at[own], load_sem.at[k]))
            stores.append(pltpu.make_async_copy(held.at[own], dst.at[own], store_sem.at[k]))
    for c in loads:
        c.start()
    for load, store in zip(loads, stores):
        load.wait()
        store.start()
    for c in stores:
        c.wait()


def local(planes, heads_dev, lin_query, lin_key, lin_value, log_decay, norm_gain,
          attn_query, attn_key, attn_value):
    rows, heads, _ = lin_query.shape
    kv_local = attn_key.shape[1]
    group = heads // kv_local
    quarter = heads // GROUP
    vmem = pl.BlockSpec(memory_space=pltpu.VMEM)
    hbm = pl.BlockSpec(memory_space=pl.ANY)
    dma = pltpu.SemaphoreType.DMA
    out = jax.ShapeDtypeStruct(lin_query.shape, BF16)
    state = (GROUP, quarter, HD, HD)
    results = pl.pallas_call(
        functools.partial(kernel, planes, heads_dev),
        out_shape=(out, out),
        in_specs=[hbm, hbm, hbm, vmem, vmem, hbm, vmem, vmem],
        out_specs=(hbm, hbm),
        scratch_shapes=[pltpu.VMEM(lin_query.shape, BF16)] * 6
        + [dma((4,)), dma((3,))]
        + [pltpu.VMEM((rows * (-(-2 * kv_local // 8) * 8), HD), F32)]
        + [
            pltpu.VMEM((rows * heads, HD), F32),
            pltpu.VMEM((rows * heads, HD), F32),
            pltpu.VMEM((rows * heads, HD), F32),
            pltpu.VMEM((rows * heads, HD), F32),
            pltpu.VMEM((2, kv_local, planes, GROUP, rows, HD), BF16),
            pltpu.VMEM((kv_local, rows * group, HD), BF16),
            pltpu.VMEM((kv_local, HD, rows * group), F32),
            pltpu.VMEM((kv_local, 1, rows * group), F32),
            pltpu.VMEM((kv_local, 1, rows * group), F32),
            pltpu.VMEM((kv_local, rows * group, HD), F32),
            pltpu.VMEM((heads, rows), F32),
            pltpu.VMEM((heads, rows, rows), F32),
            pltpu.VMEM((GROUP, heads, HD), F32),
            pltpu.VMEM(state, BF16),
            pltpu.VMEM(state, BF16),
            pltpu.VMEM(state, BF16),
            pltpu.VMEM(state, BF16),
            pltpu.VMEM(state[1:], BF16),
            pltpu.VMEM(state[1:], BF16),
            pltpu.VMEM((rows, HD), F32),
            pltpu.VMEM((max(heads_dev - 1, 1), rows, HD), F32),
        ]
        + [dma((planes,))] * 8
        + [dma] * 4
        + [dma((GROUP - 1,))] * 4
        + [dma(((GROUP - 1) * PARTS,))] * 2
        + [dma((quarter,))] * 2
        + [dma((max(heads_dev - 1, 1),))] * 2,
        compiler_params=pltpu.CompilerParams(
            collective_id=0, has_side_effects=True, vmem_limit_bytes=56 * 2**20
        ),
        name="mixers",
    )(lin_query, lin_key, lin_value, log_decay, norm_gain, attn_query,
      attn_key, attn_value)
    return pl.pallas_call(
        hand_over,
        out_shape=(out, out),
        in_specs=[hbm, hbm],
        out_specs=(hbm, hbm),
        scratch_shapes=[pltpu.VMEM(out.shape, BF16)] * 2 + [dma((8,))] * 2,
        compiler_params=pltpu.CompilerParams(vmem_limit_bytes=56 * 2**20),
        name="hand_over",
    )(*results)


def solution(mesh):
    planes = mesh.shape["ctx"] // GROUP
    return jax.shard_map(
        functools.partial(local, planes, mesh.shape["head"]),
        mesh=mesh,
        in_specs=(
            P("ctx", "head", None),
            P("ctx", "head", None),
            P("ctx", "head", None),
            P("head", "ctx"),
            P("head", None),
            P("ctx", "head", None),
            P("ctx", "head", None),
            P("ctx", "head", None),
        ),
        out_specs=(P("ctx", "head", None), P("ctx", "head", None)),
        check_vma=False,
    )
```

```python
import functools
import math

import jax
import jax.numpy as jnp
from jax import lax
from jax.experimental import pallas as pl
from jax.experimental.pallas import tpu as pltpu
from jax.sharding import PartitionSpec as P

QUERY_HEADS = 64
HD = 128
GROUP = 4
F32 = jnp.float32
BF16 = jnp.bfloat16
MESH = pl.DeviceIdType.MESH
NT = (((1,), (1,)), ((), ()))
TN = (((0,), (0,)), ((), ()))
MQ = 256
PARTS = 2


def silu(x):
    half = 0.5 * x
    return half + half * jnp.tanh(half)


def kernel(
    planes, heads_dev, lq_in, lk_in, lv_in, decay, gain, aq_in, k_in, v_in, lin_hbm, attn_hbm,
    lq, lk, lv, aq, lin_out, attn_out, in_sem, out_sem, by_row,
    qf, kf, vf, mixed, kv, qs, acc, m_ref, l_ref, ot, cum_ref, colb, lastb,
    sbuf, rs, prior, pr_send, carry, carry_out, rowsq, rowsq_in,
    z_s, z_r, zd_s, zd_r, x_s, x_r, y_s, y_r, dk_s, dk_r, dv_s, dv_r,
    s1_s, s1_r, la_s, la_r, s3_s, s3_r, c_s, c_r, h_s, h_r,
):
    loads = [
        pltpu.make_async_copy(src, dst, in_sem.at[i])
        for i, (src, dst) in enumerate(((lk_in, lk), (lv_in, lv), (aq_in, aq), (lq_in, lq)))
    ]
    for c in loads:
        c.start()
    rows, heads, _ = lq.shape
    kv_local = k_in.shape[1]
    group = heads // kv_local
    quarter = heads // GROUP
    me = lax.axis_index("ctx")
    my_head = lax.axis_index("head")
    z = me // GROUP
    p = me % GROUP
    base = z * GROUP
    px = jnp.where(p % 2 == 0, p + 1, p - 1)
    py = (p + 2) % GROUP
    pd = jnp.where(px >= 2, px - 2, px + 2)
    peers = (px, py, pd)
    has_up = z < planes - 1
    has_down = z > 0

    def remote(src, dst, s, r, ctx):
        return pltpu.make_async_remote_copy(
            src_ref=src, dst_ref=dst, send_sem=s, recv_sem=r,
            device_id={"ctx": ctx}, device_id_type=MESH,
        )

    slots = -(-2 * kv_local // 8) * 8
    both = [k_in[...].astype(F32), v_in[...].astype(F32)]
    if slots > 2 * kv_local:
        both.append(jnp.zeros((rows, slots - 2 * kv_local, HD), F32))
    by_row[...] = jnp.concatenate(both, axis=1).reshape(rows * slots, HD)
    for j in range(2):
        for g in range(kv_local):
            kv[j, g, z, p] = by_row[pl.ds(j * kv_local + g, rows, stride=slots), :].astype(BF16)

    barrier = pltpu.get_barrier_semaphore()
    for peer in peers:
        pl.semaphore_signal(barrier, inc=1, device_id={"ctx": base + peer}, device_id_type=MESH)
    for j in range(1, heads_dev):
        pl.semaphore_signal(
            barrier, inc=1, device_id={"head": (my_head + j) % heads_dev}, device_id_type=MESH
        )

    @pl.when(has_up)
    def _():
        pl.semaphore_signal(barrier, inc=1, device_id={"ctx": me + GROUP}, device_id_type=MESH)

    @pl.when(has_down)
    def _():
        pl.semaphore_signal(barrier, inc=1, device_id={"ctx": me - GROUP}, device_id_type=MESH)

    along = jnp.where(has_up, 1, 0) + jnp.where(has_down, 1, 0)
    pl.semaphore_wait(barrier, GROUP - 1 + heads_dev - 1 + along)

    def block(zz, col):
        return kv.at[:, :, zz, col]

    def up_copy(zz):
        return remote(block(zz, p), block(zz, p), z_s.at[zz], z_r.at[zz], me + GROUP)

    def up_diagonal(zz):
        return remote(block(zz, pd), block(zz, pd), zd_s.at[zz], zd_r.at[zz], me + GROUP)

    def x_copy(zz, col):
        return remote(block(zz, col), block(zz, col), x_s.at[zz], x_r.at[zz], base + px)

    def y_copy(zz, col):
        return remote(block(zz, col), block(zz, col), y_s.at[zz], y_r.at[zz], base + py)

    def dk_copy(col):
        return remote(kv.at[0, :, z, col], kv.at[0, :, z, col], dk_s, dk_r, base + py)

    def dv_copy(col):
        return remote(kv.at[1, :, z, col], kv.at[1, :, z, col], dv_s, dv_r, base + px)

    def send_in_plane(zz):
        x_copy(zz, p).start()
        y_copy(zz, p).start()

    def send_up(zz):
        @pl.when(has_up)
        def _():
            up_copy(zz).start()

    send_in_plane(z)
    send_up(z)

    step = 16

    def activate(src, dst):
        def body(i, _):
            t0 = pl.multiple_of(i * step, step)
            x = silu(src[pl.ds(t0, step)].astype(F32))
            r0 = pl.multiple_of(t0 * heads, step * heads)
            dst[pl.ds(r0, step * heads), :] = x.reshape(step * heads, HD)
            return 0

        lax.fori_loop(0, rows // step, body, 0)

    def head_rows(ref, h):
        return ref[pl.ds(h, rows, stride=heads), :]

    row_id = lax.broadcasted_iota(jnp.int32, (rows, rows), 0)
    col_id = lax.broadcasted_iota(jnp.int32, (rows, rows), 1)
    upper = jnp.where(row_id <= col_id, 1.0, 0.0).astype(F32)
    cum_all = lax.dot_general(
        decay[...], upper, (((1,), (0,)), ((), ())),
        precision=lax.Precision.HIGHEST, preferred_element_type=F32,
    )
    cum_ref[...] = cum_all
    lastb[p] = jnp.broadcast_to(cum_all[:, rows - 1 : rows], (heads, HD))
    last_copies = [
        remote(lastb.at[p], lastb.at[p], la_s.at[i], la_r.at[i], base + peer)
        for i, peer in enumerate(peers)
    ]
    for c in last_copies:
        c.start()

    loads[0].wait()
    activate(lk, kf)
    loads[1].wait()
    activate(lv, vf)

    together = min(4, quarter)

    def cum_row(h):
        return jnp.broadcast_to(cum_ref[pl.ds(h, 1), :], (rows, rows))

    def local_states(owner):
        def body(i, _):
            hs = [i * together + u for u in range(together)]
            ids = [owner * quarter + hh for hh in hs]
            ks = [head_rows(kf, h).astype(BF16).astype(F32) for h in ids]
            vs = [head_rows(vf, h).astype(BF16) for h in ids]
            lasts = [jnp.broadcast_to(lastb[p, pl.ds(h, 1), :], (rows, HD)) for h in ids]
            cols = [cum_row(h).T for h in ids]
            sks = [(k * jnp.exp(a - c)).astype(BF16) for k, a, c in zip(ks, lasts, cols)]
            sts = [
                lax.dot_general(sk, v, TN, preferred_element_type=F32) for sk, v in zip(sks, vs)
            ]
            for h, c in zip(ids, cols):
                colb[h] = c
            for hh, st in zip(hs, sts):
                sbuf[owner, hh] = st.astype(BF16)
            return 0

        lax.fori_loop(0, quarter // together, body, 0)

    s1 = [
        remote(sbuf.at[peer], rs.at[p], s1_s.at[i], s1_r.at[i], base + peer)
        for i, peer in enumerate(peers)
    ]
    for n, i in enumerate((2, 0, 1)):
        local_states(peers[i])
        s1[i].start()
        if n == 1:
            x_copy(z, px).wait_recv()
            dk_copy(px).start()
            y_copy(z, py).wait_recv()
            dv_copy(py).start()
    local_states(p)

    def next_column(r):
        @pl.when(r <= z)
        def _():
            up_copy(z - r).wait_recv()
            send_up(z - r)

    next_column(1)

    def load_queries(i, _):
        t0 = pl.multiple_of(i * step, step)
        x = aq[pl.ds(t0, step)].astype(F32)
        for g in range(kv_local):
            part = x[:, g * group : (g + 1) * group, :].reshape(step * group, HD)
            r0 = pl.multiple_of(t0 * group, step * group)
            qs[g, pl.ds(r0, step * group), :] = part.astype(BF16)
        return 0

    loads[2].wait()
    lax.fori_loop(0, rows // step, load_queries, 0)
    loads[3].wait()
    activate(lq, qf)

    def inner(i, _):
        ids = [i * together + u for u in range(together)]
        qh = [head_rows(qf, h).astype(BF16) for h in ids]
        ks = [head_rows(kf, h).astype(BF16) for h in ids]
        vs = [head_rows(vf, h).astype(BF16) for h in ids]
        spread = [colb[h] - cum_row(h) for h in ids]
        sc = [lax.dot_general(q, k, NT, preferred_element_type=F32) for q, k in zip(qh, ks)]
        dm = [jnp.exp(jnp.where(row_id >= col_id, d, -1e30)) for d in spread]
        ws = [(a * d).astype(BF16) for a, d in zip(sc, dm)]
        outs = [jnp.dot(w, v, preferred_element_type=F32) for w, v in zip(ws, vs)]
        for h, o in zip(ids, outs):
            mixed[pl.ds(h, rows, stride=heads), :] = o
        return 0

    lax.fori_loop(0, heads // together, inner, 0)

    m_ref[...] = jnp.full(m_ref.shape, -1e30, F32)
    l_ref[...] = jnp.zeros(l_ref.shape, F32)
    acc[...] = jnp.zeros(acc.shape, F32)
    scale = HD ** (-0.5) * math.log2(math.e)
    span = GROUP * rows
    tiles = rows * group // MQ

    def attend(zz, masked):
        def body(g, _):
            cols = [pl.ds(t * MQ, MQ) for t in range(tiles)]
            k = kv[0, g, zz].reshape(span, HD)
            v = kv[1, g, zz].reshape(span, HD)
            m_old = [m_ref[g, :, c] for c in cols]
            l_old = [l_ref[g, :, c] for c in cols]

            def scores(t):
                s = lax.dot_general(k, qs[g, cols[t], :], NT, preferred_element_type=F32) * scale
                if masked:
                    key_pos = lax.broadcasted_iota(jnp.int32, (span, MQ), 0)
                    col_pos = lax.broadcasted_iota(jnp.int32, (1, MQ), 1)
                    s = jnp.where(key_pos <= p * rows + (t * MQ + col_pos) // group, s, -1e30)
                return s

            def probs(t, s):
                m_new = jnp.maximum(m_old[t], jnp.max(s, axis=0, keepdims=True))
                alpha = jnp.exp2(m_old[t] - m_new)
                e = jnp.exp2(s - m_new)
                m_ref[g, :, cols[t]] = m_new
                l_ref[g, :, cols[t]] = l_old[t] * alpha + jnp.sum(e, axis=0, keepdims=True)
                return e.astype(BF16), alpha

            def values(t, e, alpha):
                o = lax.dot_general(v, e, TN, preferred_element_type=F32)
                acc[g, :, cols[t]] = acc[g, :, cols[t]] * alpha + o

            ss, es = {}, {}
            for t in range(tiles + 2):
                if t < tiles:
                    ss[t] = scores(t)
                if 0 <= t - 2 < tiles:
                    values(t - 2, *es.pop(t - 2))
                if 0 <= t - 1 < tiles:
                    es[t - 1] = probs(t - 1, ss.pop(t - 1))
            return 0

        lax.fori_loop(0, kv_local, body, 0)

    part = quarter // PARTS

    sub = 2 if part % 2 == 0 else 1
    piece = part // sub

    def carry_copy(n):
        own = pl.ds(n * piece, piece)
        return remote(carry_out.at[own], carry.at[own], c_s.at[n], c_r.at[n], me + GROUP)

    def prior_copy(j, i):
        own = pl.ds(j * part, part)
        n = j * (GROUP - 1) + i
        return remote(
            pr_send.at[peers[i], own], prior.at[p, own], s3_s.at[n], s3_r.at[n], base + peers[i]
        )

    def state_chain():
        for i in range(GROUP - 1):
            s1[i].wait_recv()
            last_copies[i].wait_recv()
        rs[p] = sbuf[p]

        @pl.when(jnp.logical_not(has_down))
        def _():
            carry[...] = jnp.zeros(carry.shape, BF16)

        for n in range(PARTS * sub):

            @pl.when(has_down)
            def _():
                carry_copy(n).wait_recv()

            for hh in range(n * piece, (n + 1) * piece):
                h = p * quarter + hh
                state = carry[hh].astype(F32)
                for i in range(GROUP):
                    pr_send[i, hh] = state.astype(BF16)
                    d = jnp.exp(lastb[i, pl.ds(h, 1), :])
                    state = d * state + rs[i, hh].astype(F32)
                carry_out[hh] = state.astype(BF16)

            @pl.when(has_up)
            def _():
                carry_copy(n).start()

            if n % sub == sub - 1:
                for i in range(GROUP - 1):
                    prior_copy(n // sub, i).start()
        prior[p] = pr_send[p]

    def turn(r, _):
        zz = z - r

        @pl.when(r < z)
        def _():
            send_in_plane(zz - 1)

        next_column(r + 2)

        @pl.when(r == 0)
        def _():
            dk_copy(pd).wait_recv()
            dv_copy(pd).wait_recv()

        @pl.when(r > 0)
        def _():
            x_copy(zz, px).wait_recv()
            y_copy(zz, py).wait_recv()
            up_diagonal(zz).wait_recv()

        @pl.when(has_up)
        def _():
            up_diagonal(zz).start()

        @pl.when(r == z)
        def _():
            state_chain()

        @pl.when(r == 0)
        def _():
            attend(zz, True)

        @pl.when(r > 0)
        def _():
            attend(zz, False)

        return 0

    lax.fori_loop(0, z + 1, turn, 0)

    for g in range(kv_local):
        for t in range(tiles):
            cols = slice(t * MQ, (t + 1) * MQ)
            ot[g, cols, :] = (acc[g, :, cols] / l_ref[g, :, cols]).T

    rowsq[...] = jnp.zeros(rowsq.shape, F32)

    def outer(owner, j):
        hs = [j * part + u for u in range(part)]
        ids = [owner * quarter + hh for hh in hs]
        qh = [head_rows(qf, h).astype(BF16) for h in ids]
        old = [head_rows(mixed, h) for h in ids]
        ps = [prior[owner, hh] for hh in hs]
        os = [jnp.dot(q, x, preferred_element_type=F32) for q, x in zip(qh, ps)]
        new = [a + o * jnp.exp(colb[h]) for a, o, h in zip(old, os, ids)]
        for h, x in zip(ids, new):
            mixed[pl.ds(h, rows, stride=heads), :] = x
        rowsq[...] += sum(x * x for x in new)

    for j in range(PARTS):
        outer(p, j)
        for i in range(GROUP - 1):
            prior_copy(j, i).wait_recv()
            outer(peers[i], j)
    h_copies = [
        pltpu.make_async_remote_copy(
            src_ref=rowsq, dst_ref=rowsq_in.at[j - 1], send_sem=h_s.at[j - 1],
            recv_sem=h_r.at[j - 1], device_id={"head": (my_head + j) % heads_dev},
            device_id_type=MESH,
        )
        for j in range(1, heads_dev)
    ]
    for c in h_copies:
        c.start()

    def store_attn(i, _):
        t0 = pl.multiple_of(i * step, step)
        r0 = pl.multiple_of(t0 * group, step * group)
        parts = [
            ot[g, pl.ds(r0, step * group), :].reshape(step, group, HD) for g in range(kv_local)
        ]
        attn_out[pl.ds(t0, step)] = jnp.concatenate(parts, axis=1).astype(BF16)
        return 0

    lax.fori_loop(0, rows // step, store_attn, 0)
    attn_store = pltpu.make_async_copy(attn_out, attn_hbm, out_sem.at[0])
    attn_store.start()

    for c in h_copies:
        c.wait_recv()
    total = rowsq[...]
    for j in range(heads_dev - 1):
        total = total + rowsq_in[j]
    mean = jnp.sum(total, axis=1, keepdims=True) / (heads_dev * heads * HD)
    for c in h_copies:
        c.wait_send()
    rowsq[...] = jnp.broadcast_to(lax.rsqrt(mean + 1e-06), (rows, HD))

    def store_lin(i, _):
        t0 = pl.multiple_of(i * step, step)
        r0 = pl.multiple_of(t0 * heads, step * heads)
        x = mixed[pl.ds(r0, step * heads), :].reshape(step, heads, HD)
        inv = rowsq[pl.ds(t0, step), :].reshape(step, 1, HD)
        lin_out[pl.ds(t0, step)] = (x * inv * gain[...][None]).astype(BF16)
        return 0

    halves = 2
    lin_stores = []
    for j in range(halves):
        n = rows // step // halves
        lax.fori_loop(j * n, (j + 1) * n, store_lin, 0)
        own = pl.ds(j * n * step, n * step)
        lin_stores.append(
            pltpu.make_async_copy(lin_out.at[own], lin_hbm.at[own], out_sem.at[1 + j])
        )
        lin_stores[j].start()

    for c in last_copies + s1:
        c.wait_send()
    for j in range(PARTS):
        for i in range(GROUP - 1):
            prior_copy(j, i).wait_send()

    @pl.when(has_up)
    def _():
        for n in range(PARTS * sub):
            carry_copy(n).wait_send()

    def drain(zz, _):
        @pl.when(has_up)
        def _():
            up_copy(zz).wait_send()
            up_diagonal(zz).wait_send()

        x_copy(zz, p).wait_send()
        y_copy(zz, p).wait_send()
        return 0

    lax.fori_loop(0, z + 1, drain, 0)
    dk_copy(px).wait_send()
    dv_copy(py).wait_send()
    attn_store.wait()
    for c in lin_stores:
        c.wait()


def hand_over(lin_in, attn_in, lin_out, attn_out, lin_held, attn_held, load_sem, store_sem):
    pieces = 4
    n = lin_in.shape[0] // pieces
    loads, stores = [], []
    arrays = ((lin_in, lin_held, lin_out), (attn_in, attn_held, attn_out))
    for i, (src, held, dst) in enumerate(arrays):
        for j in range(pieces):
            own, k = pl.ds(j * n, n), i * pieces + j
            loads.append(pltpu.make_async_copy(src.at[own], held.at[own], load_sem.at[k]))
            stores.append(pltpu.make_async_copy(held.at[own], dst.at[own], store_sem.at[k]))
    for c in loads:
        c.start()
    for load, store in zip(loads, stores):
        load.wait()
        store.start()
    for c in stores:
        c.wait()


def local(planes, heads_dev, lin_query, lin_key, lin_value, log_decay, norm_gain,
          attn_query, attn_key, attn_value):
    rows, heads, _ = lin_query.shape
    kv_local = attn_key.shape[1]
    group = heads // kv_local
    quarter = heads // GROUP
    vmem = pl.BlockSpec(memory_space=pltpu.VMEM)
    hbm = pl.BlockSpec(memory_space=pl.ANY)
    dma = pltpu.SemaphoreType.DMA
    out = jax.ShapeDtypeStruct(lin_query.shape, BF16)
    state = (GROUP, quarter, HD, HD)
    results = pl.pallas_call(
        functools.partial(kernel, planes, heads_dev),
        out_shape=(out, out),
        in_specs=[hbm, hbm, hbm, vmem, vmem, hbm, vmem, vmem],
        out_specs=(hbm, hbm),
        scratch_shapes=[pltpu.VMEM(lin_query.shape, BF16)] * 6
        + [dma((4,)), dma((3,))]
        + [pltpu.VMEM((rows * (-(-2 * kv_local // 8) * 8), HD), F32)]
        + [
            pltpu.VMEM((rows * heads, HD), F32),
            pltpu.VMEM((rows * heads, HD), F32),
            pltpu.VMEM((rows * heads, HD), F32),
            pltpu.VMEM((rows * heads, HD), F32),
            pltpu.VMEM((2, kv_local, planes, GROUP, rows, HD), BF16),
            pltpu.VMEM((kv_local, rows * group, HD), BF16),
            pltpu.VMEM((kv_local, HD, rows * group), F32),
            pltpu.VMEM((kv_local, 1, rows * group), F32),
            pltpu.VMEM((kv_local, 1, rows * group), F32),
            pltpu.VMEM((kv_local, rows * group, HD), F32),
            pltpu.VMEM((heads, rows), F32),
            pltpu.VMEM((heads, rows, rows), F32),
            pltpu.VMEM((GROUP, heads, HD), F32),
            pltpu.VMEM(state, BF16),
            pltpu.VMEM(state, BF16),
            pltpu.VMEM(state, BF16),
            pltpu.VMEM(state, BF16),
            pltpu.VMEM(state[1:], BF16),
            pltpu.VMEM(state[1:], BF16),
            pltpu.VMEM((rows, HD), F32),
            pltpu.VMEM((max(heads_dev - 1, 1), rows, HD), F32),
        ]
        + [dma((planes,))] * 8
        + [dma] * 4
        + [dma((GROUP - 1,))] * 4
        + [dma(((GROUP - 1) * PARTS,))] * 2
        + [dma((quarter,))] * 2
        + [dma((max(heads_dev - 1, 1),))] * 2,
        compiler_params=pltpu.CompilerParams(
            collective_id=0, has_side_effects=True, vmem_limit_bytes=56 * 2**20
        ),
        name="mixers",
    )(lin_query, lin_key, lin_value, log_decay, norm_gain, attn_query,
      attn_key, attn_value)
    return pl.pallas_call(
        hand_over,
        out_shape=(out, out),
        in_specs=[hbm, hbm],
        out_specs=(hbm, hbm),
        scratch_shapes=[pltpu.VMEM(out.shape, BF16)] * 2 + [dma((8,))] * 2,
        compiler_params=pltpu.CompilerParams(vmem_limit_bytes=56 * 2**20),
        name="hand_over",
    )(*results)


def solution(mesh):
    planes = mesh.shape["ctx"] // GROUP
    return jax.shard_map(
        functools.partial(local, planes, mesh.shape["head"]),
        mesh=mesh,
        in_specs=(
            P("ctx", "head", None),
            P("ctx", "head", None),
            P("ctx", "head", None),
            P("head", "ctx"),
            P("head", None),
            P("ctx", "head", None),
            P("ctx", "head", None),
            P("ctx", "head", None),
        ),
        out_specs=(P("ctx", "head", None), P("ctx", "head", None)),
        check_vma=False,
    )
```

```python
import functools
import math

import jax
import jax.numpy as jnp
from jax import lax
from jax.experimental import pallas as pl
from jax.experimental.pallas import tpu as pltpu
from jax.sharding import PartitionSpec as P

QUERY_HEADS = 64
HD = 128
GROUP = 4
F32 = jnp.float32
BF16 = jnp.bfloat16
MESH = pl.DeviceIdType.MESH
NT = (((1,), (1,)), ((), ()))
TN = (((0,), (0,)), ((), ()))
MQ = 256
PARTS = 2


def silu(x):
    half = 0.5 * x
    return half + half * jnp.tanh(half)


def kernel(
    planes, heads_dev, lq_in, lk_in, lv_in, decay, gain, aq_in, k_in, v_in, lin_hbm, attn_hbm,
    lq, lk, lv, aq, lin_out, attn_out, in_sem, out_sem, by_row,
    qf, kf, vf, mixed, kv, qs, acc, m_ref, l_ref, ot, cum_ref, colb, lastb,
    sbuf, rs, prior, pr_send, carry, carry_out, rowsq, rowsq_in,
    z_s, z_r, zd_s, zd_r, x_s, x_r, y_s, y_r, dk_s, dk_r, dv_s, dv_r,
    s1_s, s1_r, la_s, la_r, s3_s, s3_r, c_s, c_r, h_s, h_r,
):
    loads = [
        pltpu.make_async_copy(src, dst, in_sem.at[i])
        for i, (src, dst) in enumerate(((lk_in, lk), (lv_in, lv), (aq_in, aq), (lq_in, lq)))
    ]
    for c in loads:
        c.start()
    rows, heads, _ = lq.shape
    kv_local = k_in.shape[1]
    group = heads // kv_local
    quarter = heads // GROUP
    me = lax.axis_index("ctx")
    my_head = lax.axis_index("head")
    z = me // GROUP
    p = me % GROUP
    base = z * GROUP
    px = jnp.where(p % 2 == 0, p + 1, p - 1)
    py = (p + 2) % GROUP
    pd = jnp.where(px >= 2, px - 2, px + 2)
    peers = (px, py, pd)
    has_up = z < planes - 1
    has_down = z > 0

    def remote(src, dst, s, r, ctx):
        return pltpu.make_async_remote_copy(
            src_ref=src, dst_ref=dst, send_sem=s, recv_sem=r,
            device_id={"ctx": ctx}, device_id_type=MESH,
        )

    slots = -(-2 * kv_local // 8) * 8
    both = [k_in[...].astype(F32), v_in[...].astype(F32)]
    if slots > 2 * kv_local:
        both.append(jnp.zeros((rows, slots - 2 * kv_local, HD), F32))
    by_row[...] = jnp.concatenate(both, axis=1).reshape(rows * slots, HD)
    for j in range(2):
        for g in range(kv_local):
            kv[j, g, z, p] = by_row[pl.ds(j * kv_local + g, rows, stride=slots), :].astype(BF16)

    barrier = pltpu.get_barrier_semaphore()
    for peer in peers:
        pl.semaphore_signal(barrier, inc=1, device_id={"ctx": base + peer}, device_id_type=MESH)
    for j in range(1, heads_dev):
        pl.semaphore_signal(
            barrier, inc=1, device_id={"head": (my_head + j) % heads_dev}, device_id_type=MESH
        )

    @pl.when(has_up)
    def _():
        pl.semaphore_signal(barrier, inc=1, device_id={"ctx": me + GROUP}, device_id_type=MESH)

    @pl.when(has_down)
    def _():
        pl.semaphore_signal(barrier, inc=1, device_id={"ctx": me - GROUP}, device_id_type=MESH)

    along = jnp.where(has_up, 1, 0) + jnp.where(has_down, 1, 0)
    pl.semaphore_wait(barrier, GROUP - 1 + heads_dev - 1 + along)

    def block(zz, col):
        return kv.at[:, :, zz, col]

    def up_copy(zz):
        return remote(block(zz, p), block(zz, p), z_s.at[zz], z_r.at[zz], me + GROUP)

    def up_diagonal(zz):
        return remote(block(zz, pd), block(zz, pd), zd_s.at[zz], zd_r.at[zz], me + GROUP)

    def x_copy(zz, col):
        return remote(block(zz, col), block(zz, col), x_s.at[zz], x_r.at[zz], base + px)

    def y_copy(zz, col):
        return remote(block(zz, col), block(zz, col), y_s.at[zz], y_r.at[zz], base + py)

    def dk_copy(col):
        return remote(kv.at[0, :, z, col], kv.at[0, :, z, col], dk_s, dk_r, base + py)

    def dv_copy(col):
        return remote(kv.at[1, :, z, col], kv.at[1, :, z, col], dv_s, dv_r, base + px)

    def send_in_plane(zz):
        x_copy(zz, p).start()
        y_copy(zz, p).start()

    def send_up(zz):
        @pl.when(has_up)
        def _():
            up_copy(zz).start()

    send_in_plane(z)
    send_up(z)

    step = 16

    def activate(src, dst):
        def body(i, _):
            t0 = pl.multiple_of(i * step, step)
            x = silu(src[pl.ds(t0, step)].astype(F32))
            r0 = pl.multiple_of(t0 * heads, step * heads)
            dst[pl.ds(r0, step * heads), :] = x.reshape(step * heads, HD)
            return 0

        lax.fori_loop(0, rows // step, body, 0)

    def head_rows(ref, h):
        return ref[pl.ds(h, rows, stride=heads), :]

    row_id = lax.broadcasted_iota(jnp.int32, (rows, rows), 0)
    col_id = lax.broadcasted_iota(jnp.int32, (rows, rows), 1)
    upper = jnp.where(row_id <= col_id, 1.0, 0.0).astype(F32)
    cum_all = lax.dot_general(
        decay[...], upper, (((1,), (0,)), ((), ())),
        precision=lax.Precision.HIGHEST, preferred_element_type=F32,
    )
    cum_ref[...] = cum_all
    lastb[p] = jnp.broadcast_to(cum_all[:, rows - 1 : rows], (heads, HD))
    last_copies = [
        remote(lastb.at[p], lastb.at[p], la_s.at[i], la_r.at[i], base + peer)
        for i, peer in enumerate(peers)
    ]
    for c in last_copies:
        c.start()

    loads[0].wait()
    activate(lk, kf)
    loads[1].wait()
    activate(lv, vf)

    together = min(4, quarter)

    def cum_row(h):
        return jnp.broadcast_to(cum_ref[pl.ds(h, 1), :], (rows, rows))

    def local_states(owner):
        def body(i, _):
            hs = [i * together + u for u in range(together)]
            ids = [owner * quarter + hh for hh in hs]
            ks = [head_rows(kf, h).astype(BF16).astype(F32) for h in ids]
            vs = [head_rows(vf, h).astype(BF16) for h in ids]
            lasts = [jnp.broadcast_to(lastb[p, pl.ds(h, 1), :], (rows, HD)) for h in ids]
            cols = [cum_row(h).T for h in ids]
            sks = [(k * jnp.exp(a - c)).astype(BF16) for k, a, c in zip(ks, lasts, cols)]
            sts = [
                lax.dot_general(sk, v, TN, preferred_element_type=F32) for sk, v in zip(sks, vs)
            ]
            for h, c in zip(ids, cols):
                colb[h] = c
            for hh, st in zip(hs, sts):
                sbuf[owner, hh] = st.astype(BF16)
            return 0

        lax.fori_loop(0, quarter // together, body, 0)

    s1 = [
        remote(sbuf.at[peer], rs.at[p], s1_s.at[i], s1_r.at[i], base + peer)
        for i, peer in enumerate(peers)
    ]
    for peer, c in zip(peers, s1):
        local_states(peer)
        c.start()
    local_states(p)

    def next_column(r):
        @pl.when(r <= z)
        def _():
            up_copy(z - r).wait_recv()
            send_up(z - r)

    x_copy(z, px).wait_recv()
    dk_copy(px).start()
    y_copy(z, py).wait_recv()
    dv_copy(py).start()
    next_column(1)

    def load_queries(i, _):
        t0 = pl.multiple_of(i * step, step)
        x = aq[pl.ds(t0, step)].astype(F32)
        for g in range(kv_local):
            part = x[:, g * group : (g + 1) * group, :].reshape(step * group, HD)
            r0 = pl.multiple_of(t0 * group, step * group)
            qs[g, pl.ds(r0, step * group), :] = part.astype(BF16)
        return 0

    loads[2].wait()
    lax.fori_loop(0, rows // step, load_queries, 0)
    loads[3].wait()
    activate(lq, qf)

    def inner(i, _):
        ids = [i * together + u for u in range(together)]
        qh = [head_rows(qf, h).astype(BF16) for h in ids]
        ks = [head_rows(kf, h).astype(BF16) for h in ids]
        vs = [head_rows(vf, h).astype(BF16) for h in ids]
        spread = [colb[h] - cum_row(h) for h in ids]
        sc = [lax.dot_general(q, k, NT, preferred_element_type=F32) for q, k in zip(qh, ks)]
        dm = [jnp.exp(jnp.where(row_id >= col_id, d, -1e30)) for d in spread]
        ws = [(a * d).astype(BF16) for a, d in zip(sc, dm)]
        outs = [jnp.dot(w, v, preferred_element_type=F32) for w, v in zip(ws, vs)]
        for h, o in zip(ids, outs):
            mixed[pl.ds(h, rows, stride=heads), :] = o
        return 0

    lax.fori_loop(0, heads // together, inner, 0)

    m_ref[...] = jnp.full(m_ref.shape, -1e30, F32)
    l_ref[...] = jnp.zeros(l_ref.shape, F32)
    acc[...] = jnp.zeros(acc.shape, F32)
    scale = HD ** (-0.5) * math.log2(math.e)
    span = GROUP * rows
    tiles = rows * group // MQ

    def attend(zz, masked):
        def body(g, _):
            cols = [pl.ds(t * MQ, MQ) for t in range(tiles)]
            k = kv[0, g, zz].reshape(span, HD)
            v = kv[1, g, zz].reshape(span, HD)
            m_old = [m_ref[g, :, c] for c in cols]
            l_old = [l_ref[g, :, c] for c in cols]

            def scores(t):
                s = lax.dot_general(k, qs[g, cols[t], :], NT, preferred_element_type=F32) * scale
                if masked:
                    key_pos = lax.broadcasted_iota(jnp.int32, (span, MQ), 0)
                    col_pos = lax.broadcasted_iota(jnp.int32, (1, MQ), 1)
                    s = jnp.where(key_pos <= p * rows + (t * MQ + col_pos) // group, s, -1e30)
                return s

            def probs(t, s):
                m_new = jnp.maximum(m_old[t], jnp.max(s, axis=0, keepdims=True))
                alpha = jnp.exp2(m_old[t] - m_new)
                e = jnp.exp2(s - m_new)
                m_ref[g, :, cols[t]] = m_new
                l_ref[g, :, cols[t]] = l_old[t] * alpha + jnp.sum(e, axis=0, keepdims=True)
                return e.astype(BF16), alpha

            def values(t, e, alpha):
                o = lax.dot_general(v, e, TN, preferred_element_type=F32)
                acc[g, :, cols[t]] = acc[g, :, cols[t]] * alpha + o

            ss, es = {}, {}
            for t in range(tiles + 2):
                if t < tiles:
                    ss[t] = scores(t)
                if 0 <= t - 2 < tiles:
                    values(t - 2, *es.pop(t - 2))
                if 0 <= t - 1 < tiles:
                    es[t - 1] = probs(t - 1, ss.pop(t - 1))
            return 0

        lax.fori_loop(0, kv_local, body, 0)

    part = quarter // PARTS

    sub = 2 if part % 2 == 0 else 1
    piece = part // sub

    def carry_copy(n):
        own = pl.ds(n * piece, piece)
        return remote(carry_out.at[own], carry.at[own], c_s.at[n], c_r.at[n], me + GROUP)

    def prior_copy(j, i):
        own = pl.ds(j * part, part)
        n = j * (GROUP - 1) + i
        return remote(
            pr_send.at[peers[i], own], prior.at[p, own], s3_s.at[n], s3_r.at[n], base + peers[i]
        )

    def state_chain():
        for i in range(GROUP - 1):
            s1[i].wait_recv()
            last_copies[i].wait_recv()
        rs[p] = sbuf[p]

        @pl.when(jnp.logical_not(has_down))
        def _():
            carry[...] = jnp.zeros(carry.shape, BF16)

        for n in range(PARTS * sub):

            @pl.when(has_down)
            def _():
                carry_copy(n).wait_recv()

            for hh in range(n * piece, (n + 1) * piece):
                h = p * quarter + hh
                state = carry[hh].astype(F32)
                for i in range(GROUP):
                    pr_send[i, hh] = state.astype(BF16)
                    d = jnp.exp(lastb[i, pl.ds(h, 1), :])
                    state = d * state + rs[i, hh].astype(F32)
                carry_out[hh] = state.astype(BF16)

            @pl.when(has_up)
            def _():
                carry_copy(n).start()

            if n % sub == sub - 1:
                for i in range(GROUP - 1):
                    prior_copy(n // sub, i).start()
        prior[p] = pr_send[p]

    def turn(r, _):
        zz = z - r

        @pl.when(r < z)
        def _():
            send_in_plane(zz - 1)

        next_column(r + 2)

        @pl.when(z == 0)
        def _():
            state_chain()

        @pl.when(r == 0)
        def _():
            dk_copy(pd).wait_recv()
            dv_copy(pd).wait_recv()

        @pl.when(r > 0)
        def _():
            x_copy(zz, px).wait_recv()
            y_copy(zz, py).wait_recv()
            up_diagonal(zz).wait_recv()

        @pl.when(has_up)
        def _():
            up_diagonal(zz).start()

        @pl.when(jnp.logical_and(r == z, z > 0))
        def _():
            state_chain()

        @pl.when(r == 0)
        def _():
            attend(zz, True)

        @pl.when(r > 0)
        def _():
            attend(zz, False)

        return 0

    lax.fori_loop(0, z + 1, turn, 0)

    for g in range(kv_local):
        for t in range(tiles):
            cols = slice(t * MQ, (t + 1) * MQ)
            ot[g, cols, :] = (acc[g, :, cols] / l_ref[g, :, cols]).T

    rowsq[...] = jnp.zeros(rowsq.shape, F32)

    def outer(owner, j):
        hs = [j * part + u for u in range(part)]
        ids = [owner * quarter + hh for hh in hs]
        qh = [head_rows(qf, h).astype(BF16) for h in ids]
        old = [head_rows(mixed, h) for h in ids]
        ps = [prior[owner, hh] for hh in hs]
        os = [jnp.dot(q, x, preferred_element_type=F32) for q, x in zip(qh, ps)]
        new = [a + o * jnp.exp(colb[h]) for a, o, h in zip(old, os, ids)]
        for h, x in zip(ids, new):
            mixed[pl.ds(h, rows, stride=heads), :] = x
        rowsq[...] += sum(x * x for x in new)

    for j in range(PARTS):
        outer(p, j)
        for i in range(GROUP - 1):
            prior_copy(j, i).wait_recv()
            outer(peers[i], j)
    h_copies = [
        pltpu.make_async_remote_copy(
            src_ref=rowsq, dst_ref=rowsq_in.at[j - 1], send_sem=h_s.at[j - 1],
            recv_sem=h_r.at[j - 1], device_id={"head": (my_head + j) % heads_dev},
            device_id_type=MESH,
        )
        for j in range(1, heads_dev)
    ]
    for c in h_copies:
        c.start()

    def store_attn(i, _):
        t0 = pl.multiple_of(i * step, step)
        r0 = pl.multiple_of(t0 * group, step * group)
        parts = [
            ot[g, pl.ds(r0, step * group), :].reshape(step, group, HD) for g in range(kv_local)
        ]
        attn_out[pl.ds(t0, step)] = jnp.concatenate(parts, axis=1).astype(BF16)
        return 0

    lax.fori_loop(0, rows // step, store_attn, 0)
    attn_store = pltpu.make_async_copy(attn_out, attn_hbm, out_sem.at[0])
    attn_store.start()

    for c in h_copies:
        c.wait_recv()
    total = rowsq[...]
    for j in range(heads_dev - 1):
        total = total + rowsq_in[j]
    mean = jnp.sum(total, axis=1, keepdims=True) / (heads_dev * heads * HD)
    for c in h_copies:
        c.wait_send()
    rowsq[...] = jnp.broadcast_to(lax.rsqrt(mean + 1e-06), (rows, HD))

    def store_lin(i, _):
        t0 = pl.multiple_of(i * step, step)
        r0 = pl.multiple_of(t0 * heads, step * heads)
        x = mixed[pl.ds(r0, step * heads), :].reshape(step, heads, HD)
        inv = rowsq[pl.ds(t0, step), :].reshape(step, 1, HD)
        lin_out[pl.ds(t0, step)] = (x * inv * gain[...][None]).astype(BF16)
        return 0

    halves = 2
    lin_stores = []
    for j in range(halves):
        n = rows // step // halves
        lax.fori_loop(j * n, (j + 1) * n, store_lin, 0)
        own = pl.ds(j * n * step, n * step)
        lin_stores.append(
            pltpu.make_async_copy(lin_out.at[own], lin_hbm.at[own], out_sem.at[1 + j])
        )
        lin_stores[j].start()

    for c in last_copies + s1:
        c.wait_send()
    for j in range(PARTS):
        for i in range(GROUP - 1):
            prior_copy(j, i).wait_send()

    @pl.when(has_up)
    def _():
        for n in range(PARTS * sub):
            carry_copy(n).wait_send()

    def drain(zz, _):
        @pl.when(has_up)
        def _():
            up_copy(zz).wait_send()
            up_diagonal(zz).wait_send()

        x_copy(zz, p).wait_send()
        y_copy(zz, p).wait_send()
        return 0

    lax.fori_loop(0, z + 1, drain, 0)
    dk_copy(px).wait_send()
    dv_copy(py).wait_send()
    attn_store.wait()
    for c in lin_stores:
        c.wait()


def hand_over(lin_in, attn_in, lin_out, attn_out, lin_held, attn_held, load_sem, store_sem):
    pieces = 4
    n = lin_in.shape[0] // pieces
    loads, stores = [], []
    arrays = ((lin_in, lin_held, lin_out), (attn_in, attn_held, attn_out))
    for i, (src, held, dst) in enumerate(arrays):
        for j in range(pieces):
            own, k = pl.ds(j * n, n), i * pieces + j
            loads.append(pltpu.make_async_copy(src.at[own], held.at[own], load_sem.at[k]))
            stores.append(pltpu.make_async_copy(held.at[own], dst.at[own], store_sem.at[k]))
    for c in loads:
        c.start()
    for load, store in zip(loads, stores):
        load.wait()
        store.start()
    for c in stores:
        c.wait()


def local(planes, heads_dev, lin_query, lin_key, lin_value, log_decay, norm_gain,
          attn_query, attn_key, attn_value):
    rows, heads, _ = lin_query.shape
    kv_local = attn_key.shape[1]
    group = heads // kv_local
    quarter = heads // GROUP
    vmem = pl.BlockSpec(memory_space=pltpu.VMEM)
    hbm = pl.BlockSpec(memory_space=pl.ANY)
    dma = pltpu.SemaphoreType.DMA
    out = jax.ShapeDtypeStruct(lin_query.shape, BF16)
    state = (GROUP, quarter, HD, HD)
    results = pl.pallas_call(
        functools.partial(kernel, planes, heads_dev),
        out_shape=(out, out),
        in_specs=[hbm, hbm, hbm, vmem, vmem, hbm, vmem, vmem],
        out_specs=(hbm, hbm),
        scratch_shapes=[pltpu.VMEM(lin_query.shape, BF16)] * 6
        + [dma((4,)), dma((3,))]
        + [pltpu.VMEM((rows * (-(-2 * kv_local // 8) * 8), HD), F32)]
        + [
            pltpu.VMEM((rows * heads, HD), F32),
            pltpu.VMEM((rows * heads, HD), F32),
            pltpu.VMEM((rows * heads, HD), F32),
            pltpu.VMEM((rows * heads, HD), F32),
            pltpu.VMEM((2, kv_local, planes, GROUP, rows, HD), BF16),
            pltpu.VMEM((kv_local, rows * group, HD), BF16),
            pltpu.VMEM((kv_local, HD, rows * group), F32),
            pltpu.VMEM((kv_local, 1, rows * group), F32),
            pltpu.VMEM((kv_local, 1, rows * group), F32),
            pltpu.VMEM((kv_local, rows * group, HD), F32),
            pltpu.VMEM((heads, rows), F32),
            pltpu.VMEM((heads, rows, rows), F32),
            pltpu.VMEM((GROUP, heads, HD), F32),
            pltpu.VMEM(state, BF16),
            pltpu.VMEM(state, BF16),
            pltpu.VMEM(state, BF16),
            pltpu.VMEM(state, BF16),
            pltpu.VMEM(state[1:], BF16),
            pltpu.VMEM(state[1:], BF16),
            pltpu.VMEM((rows, HD), F32),
            pltpu.VMEM((max(heads_dev - 1, 1), rows, HD), F32),
        ]
        + [dma((planes,))] * 8
        + [dma] * 4
        + [dma((GROUP - 1,))] * 4
        + [dma(((GROUP - 1) * PARTS,))] * 2
        + [dma((quarter,))] * 2
        + [dma((max(heads_dev - 1, 1),))] * 2,
        compiler_params=pltpu.CompilerParams(
            collective_id=0, has_side_effects=True, vmem_limit_bytes=56 * 2**20
        ),
        name="mixers",
    )(lin_query, lin_key, lin_value, log_decay, norm_gain, attn_query,
      attn_key, attn_value)
    return pl.pallas_call(
        hand_over,
        out_shape=(out, out),
        in_specs=[hbm, hbm],
        out_specs=(hbm, hbm),
        scratch_shapes=[pltpu.VMEM(out.shape, BF16)] * 2 + [dma((8,))] * 2,
        compiler_params=pltpu.CompilerParams(vmem_limit_bytes=56 * 2**20),
        name="hand_over",
    )(*results)


def solution(mesh):
    planes = mesh.shape["ctx"] // GROUP
    return jax.shard_map(
        functools.partial(local, planes, mesh.shape["head"]),
        mesh=mesh,
        in_specs=(
            P("ctx", "head", None),
            P("ctx", "head", None),
            P("ctx", "head", None),
            P("head", "ctx"),
            P("head", None),
            P("ctx", "head", None),
            P("ctx", "head", None),
            P("ctx", "head", None),
        ),
        out_specs=(P("ctx", "head", None), P("ctx", "head", None)),
        check_vma=False,
    )
```
